32 devices in a mesh: gx: 4 (over y, x), gy: 4 (over z), gz: 2 (over core).
Axes of the slice: x: 2, y: 2, z: 4, core: 2. Of those that a mesh axis runs over, the one named last changes fastest.
Arguments:
- conserved: float32 [14, 32, 256, 512], P(None, 'gx', 'gy', 'gz')
- char_left: float32 [14, 14], replicated
- char_right: float32 [14, 14], replicated
- shock_list: int32 [4, 4, 2, 128], P('gx', 'gy', 'gz'), may hold values from 0 to 511, as said below
- shock_count: int32 [4, 4, 2], P('gx', 'gy', 'gz'), may hold values from 32 to 128, as said below
Outputs:
- advanced: float32 [14, 32, 256, 512], P(None, 'gx', 'gy', 'gz')
The draws below stay inside these ranges and needn't reach their ends.
Inputs may be any that keep to these rules, and one draw needn't show every extreme that they name: `shock_list`: the entries of one device's list are distinct local pencil indices; only the first shock_count of them are shocked pencils. `shock_count`: in every column of devices along gx (fixed gy and gz index) one device has 128 shocked pencils and every other device has 32, so a column holds 224 in all.
All inputs are finite; a program needn't handle non-finite values.
Results may differ from the reference program's by a relative error of at most 0.00005.
Values sent between devices are 32-bit elements; how exact they have to be, the bound alone decides.
No kernel may reach another device: no remote copies, remote signals or barrier semaphores. Data moves between devices by JAX's collectives and lax.ppermute only.
A program may use at most 192 MiB of HBM per device.

```python
import math
import jax
import jax.numpy as jnp
from jax import lax

SPECIES = 9
VARIABLES = 14
CX = 8
CY = 64
CZ = 256
SHOCK_MAX = 128
NX = 32
NY = 256
NZ = 512
N_GX = 4
N_GY = 4
N_GZ = 2


def draw_conserved(key, part):
    grid_shape = (NX, NY, NZ)
    subkeys = jax.random.split(key, 4)
    species = jnp.exp(jax.random.uniform(subkeys[0], (SPECIES,) + grid_shape, jnp.float32, math.log(0.05), math.log(0.5)))
    momenta = jnp.clip(jax.random.normal(subkeys[1], (3,) + grid_shape, jnp.float32), -3.0, 3.0)
    energy = jax.random.uniform(subkeys[2], (1,) + grid_shape, jnp.float32, 2.5, 5.0)
    vibration = jax.random.uniform(subkeys[3], (1,) + grid_shape, jnp.float32, 0.1, 0.8)
    return jnp.concatenate([species, momenta, energy, vibration], axis=0)


def basis_matrix(key, salt):
    inner_key = jax.random.fold_in(key, salt)
    noise = jax.random.normal(inner_key, (VARIABLES, VARIABLES), jnp.float32)
    return jnp.eye(VARIABLES, dtype=jnp.float32) + 0.3 / math.sqrt(VARIABLES) * noise


def draw_char_left(key, part):
    return basis_matrix(key, 31)


def draw_char_right(key, part):
    return basis_matrix(key, 57)


def draw_shock_list(key, part):
    pencil_total = CX * CY
    scores = jax.random.randint(jax.random.fold_in(key, 11), (N_GX, N_GY, N_GZ, pencil_total), 0, 1 << 16)
    distinct = scores * pencil_total + jnp.arange(pencil_total, dtype=jnp.int32)
    ordering = jnp.argsort(distinct, axis=-1)
    return ordering[..., :SHOCK_MAX].astype(jnp.int32)


def draw_shock_count(key, part):
    front = jax.random.randint(jax.random.fold_in(key, 23), (1, N_GY, N_GZ), 0, N_GX)
    column = jnp.arange(N_GX, dtype=jnp.int32)[:, None, None]
    return jnp.where(column == front, SHOCK_MAX, SHOCK_MAX // 4).astype(jnp.int32)


def setup_inputs(seed: int = 0) -> dict:
    arg_keys = jax.random.split(jax.random.key(seed), 6)
    conserved = draw_conserved(jax.random.fold_in(arg_keys[5], 71), 0)
    char_left = draw_char_left(jax.random.fold_in(arg_keys[5], 71), 0)
    char_right = draw_char_right(jax.random.fold_in(arg_keys[5], 71), 0)
    shock_list = draw_shock_list(jax.random.fold_in(arg_keys[5], 71), 0)
    shock_count = draw_shock_count(jax.random.fold_in(arg_keys[5], 71), 0)
    return {"conserved": conserved, "char_left": char_left, "char_right": char_right, "shock_list": shock_list, "shock_count": shock_count}


gas_excess = 0.4
time_step = 0.2
weno_epsilon = 1e-6


def directed_flux(values_in, normal):
    density = jnp.sum(values_in[:SPECIES], axis=0)
    inverse = 1.0 / density
    velocity = values_in[SPECIES + normal] * inverse
    momenta = values_in[SPECIES:SPECIES + 3]
    kinetic = 0.5 * jnp.sum(momenta * momenta, axis=0) * inverse
    pressure = gas_excess * (values_in[SPECIES + 3] - values_in[SPECIES + 4] - kinetic)
    result = values_in * velocity[None]
    result = result.at[SPECIES + normal].add(pressure)
    result = result.at[SPECIES + 3].add(pressure * velocity)
    return result


def central_difference(values_in, dimension, length_cells):
    def shifted(begin_at):
        return lax.slice_in_dim(values_in, begin_at, begin_at + length_cells, axis=dimension)
    return (45.0 * (shifted(4) - shifted(2)) - 9.0 * (shifted(5) - shifted(1)) + (shifted(6) - shifted(0))) / 60.0


def upwind_value(first_cell, second_cell, middle, fourth_cell, fifth_cell):
    stencil_zero = (2.0 * first_cell - 7.0 * second_cell + 11.0 * middle) / 6.0
    stencil_one = (-second_cell + 5.0 * middle + 2.0 * fourth_cell) / 6.0
    stencil_two = (2.0 * middle + 5.0 * fourth_cell - fifth_cell) / 6.0
    smooth_zero = 13.0 / 12.0 * (first_cell - 2.0 * second_cell + middle) ** 2 + 0.25 * (first_cell - 4.0 * second_cell + 3.0 * middle) ** 2
    smooth_one = 13.0 / 12.0 * (second_cell - 2.0 * middle + fourth_cell) ** 2 + 0.25 * (second_cell - fourth_cell) ** 2
    smooth_two = 13.0 / 12.0 * (middle - 2.0 * fourth_cell + fifth_cell) ** 2 + 0.25 * (3.0 * middle - 4.0 * fourth_cell + fifth_cell) ** 2
    weight_zero = 0.1 / (weno_epsilon + smooth_zero) ** 2
    weight_one = 0.6 / (weno_epsilon + smooth_one) ** 2
    weight_two = 0.3 / (weno_epsilon + smooth_two) ** 2
    return (weight_zero * stencil_zero + weight_one * stencil_one + weight_two * stencil_two) / (weight_zero + weight_one + weight_two)


def weno_divergence(pencils, char_left, char_right):
    fluxes = directed_flux(pencils, 2)
    density = jnp.sum(pencils[:SPECIES], axis=0)
    wave_speed = jnp.max(jnp.abs(pencils[SPECIES + 2] / density), axis=-1) + 1.0
    outward = 0.5 * (fluxes + wave_speed[None, :, None] * pencils)
    inward = 0.5 * (fluxes - wave_speed[None, :, None] * pencils)
    char_out = jnp.einsum("ij,jpk->ipk", char_left, outward, precision=lax.Precision.HIGHEST)
    char_in = jnp.einsum("ij,jpk->ipk", char_left, inward, precision=lax.Precision.HIGHEST)
    face_count = pencils.shape[-1] - 5

    def window(values_in, begin_at):
        return values_in[..., begin_at:begin_at + face_count]

    summed = upwind_value(window(char_out, 0), window(char_out, 1), window(char_out, 2), window(char_out, 3), window(char_out, 4))
    summed = summed + upwind_value(window(char_in, 5), window(char_in, 4), window(char_in, 3), window(char_in, 2), window(char_in, 1))
    face_values = jnp.einsum("ij,jpk->ipk", char_right, summed, precision=lax.Precision.HIGHEST)
    return face_values[..., 1:] - face_values[..., :-1]


def reference(conserved, char_left, char_right, shock_list, shock_count):
    def plane_terms(x_plane):
        along_y = jnp.concatenate([x_plane[:, -3:], x_plane, x_plane[:, :3]], axis=1)
        along_z = jnp.concatenate([x_plane[:, :, -3:], x_plane, x_plane[:, :, :3]], axis=2)
        y_term = central_difference(directed_flux(along_y, 1), 1, NY)
        z_term = central_difference(directed_flux(along_z, 2), 2, NZ)

        def arrange(term):
            return jnp.transpose(term.reshape(VARIABLES, NY, N_GZ, CZ), (1, 2, 0, 3))
        return arrange(y_term), arrange(z_term)

    y_all, z_all = lax.map(plane_terms, jnp.moveaxis(conserved, 1, 0))
    block_x = jnp.arange(N_GX, dtype=jnp.int32)[:, None, None, None]
    block_y = jnp.arange(N_GY, dtype=jnp.int32)[None, :, None, None]
    block_z = jnp.arange(N_GZ, dtype=jnp.int32)[None, None, :, None]
    slot_index = jnp.arange(SHOCK_MAX, dtype=jnp.int32)[None, None, None, :]
    in_list = slot_index < shock_count[..., None]
    pencil_x = (block_x * CX + shock_list // CY).astype(jnp.int32)
    pencil_y = (block_y * CY + shock_list % CY).astype(jnp.int32)
    pencil_z = (block_z + 0 * shock_list).astype(jnp.int32)
    target_x = jnp.where(in_list, pencil_x, NX).reshape(-1).astype(jnp.int32)
    pencil_x = pencil_x.reshape(-1)
    pencil_y = pencil_y.reshape(-1)
    pencil_z = pencil_z.reshape(-1)
    offsets = jnp.arange(-3, CZ + 3, dtype=jnp.int32)
    z_cells = ((pencil_z[:, None] * CZ + offsets[None, :]) % NZ).astype(jnp.int32)
    pencils = conserved[:, pencil_x[:, None], pencil_y[:, None], z_cells]
    weno_terms = weno_divergence(pencils, char_left, char_right)
    z_all = z_all.at[target_x, pencil_y, pencil_z].set(jnp.transpose(weno_terms, (1, 0, 2)), mode="drop")
    combined = jnp.transpose(y_all + z_all, (3, 0, 1, 2, 4)).reshape(VARIABLES, NX, NY, NZ)
    return conserved - time_step * combined
```

```python
import functools

import jax
import jax.numpy as jnp
from jax import lax
from jax.experimental import pallas as pl
from jax.experimental.pallas import tpu as pltpu
from jax.sharding import PartitionSpec as P

SPECIES = 9
VARIABLES = 14
WIDTH = 3
GROUP = 16
LANES = 128
LEAD = 8

gas_excess = 0.4
time_step = 0.2
weno_epsilon = 1e-06

F32 = jnp.float32
BF16 = jnp.bfloat16


def split(values):
    high = values.astype(BF16)
    low = (values - high.astype(F32)).astype(BF16)
    return high, low


def dot(left, right):
    return jnp.dot(left, right, preferred_element_type=F32)


def state_of(parts):
    density = parts[0]
    for index in range(1, SPECIES):
        density = density + parts[index]
    inverse = pl.reciprocal(density, approx=True)
    first, second, last = parts[SPECIES], parts[SPECIES + 1], parts[SPECIES + 2]
    kinetic = 0.5 * (first * first + second * second + last * last) * inverse
    pressure = gas_excess * (parts[SPECIES + 3] - parts[SPECIES + 4] - kinetic)
    return inverse, pressure


def flux_of(parts, normal):
    inverse, pressure = state_of(parts)
    velocity = parts[SPECIES + normal] * inverse
    result = [part * velocity for part in parts]
    result[SPECIES + normal] = result[SPECIES + normal] + pressure
    result[SPECIES + 3] = result[SPECIES + 3] + pressure * velocity
    return result


def pack_y_kernel(u_ref, tail_ref, head_ref, sem):
    cells_x, cells_y = u_ref.shape[1], u_ref.shape[2]
    for x in range(cells_x):
        for j in range(WIDTH):
            pltpu.make_async_copy(
                u_ref.at[:, x, pl.ds(cells_y - WIDTH + j, 1), :], tail_ref.at[j, :, pl.ds(x, 1), :], sem
            ).start()
            pltpu.make_async_copy(
                u_ref.at[:, x, pl.ds(j, 1), :], head_ref.at[j, :, pl.ds(x, 1), :], sem
            ).start()
    pltpu.make_async_copy(tail_ref, tail_ref, sem).wait()
    pltpu.make_async_copy(head_ref, head_ref, sem).wait()


def pack_y(conserved):
    cells_x, cells_z = conserved.shape[1], conserved.shape[3]
    face = jax.ShapeDtypeStruct((WIDTH, VARIABLES, cells_x, cells_z), F32)
    return pl.pallas_call(
        pack_y_kernel,
        out_shape=[face, face],
        in_specs=[pl.BlockSpec(memory_space=pl.ANY)],
        out_specs=[pl.BlockSpec(memory_space=pltpu.VMEM)] * 2,
        scratch_shapes=[pltpu.SemaphoreType.DMA(())],
        cost_estimate=pl.CostEstimate(flops=0, bytes_accessed=2_000_000, transcendentals=0),
        name="pack_y",
    )(conserved)


def pack_z_kernel(u_ref, out_ref):
    cells_z = u_ref.shape[3]
    lane = lax.broadcasted_iota(jnp.int32, (u_ref.shape[2], LANES), 1)
    packed = jnp.zeros((u_ref.shape[2], LANES), F32)
    for v in range(VARIABLES):
        both = jnp.where(lane < LANES // 2, u_ref[v, 0, :, :LANES], u_ref[v, 0, :, cells_z - LANES :])
        packed = jnp.where(lane >> 3 == v, pltpu.roll(both, 8 * v + WIDTH, 1), packed)
    out_ref[...] = packed


def pack_z(conserved):
    _, cells_x, cells_y, cells_z = conserved.shape
    return pl.pallas_call(
        pack_z_kernel,
        out_shape=jax.ShapeDtypeStruct((cells_x * cells_y, LANES), F32),
        grid=(cells_x,),
        in_specs=[pl.BlockSpec((VARIABLES, 1, cells_y, cells_z), lambda x: (0, x, 0, 0))],
        out_specs=pl.BlockSpec((cells_y, LANES), lambda x: (x, 0)),
        compiler_params=pltpu.CompilerParams(vmem_limit_bytes=16 << 20),
        cost_estimate=pl.CostEstimate(flops=4_000_000, bytes_accessed=7_600_000, transcendentals=0),
        name="pack_z",
    )(conserved)


def exchange_z(packed):
    count = lax.axis_size("gz")
    if count == 1:
        return packed
    ahead = [(i, (i + 1) % count) for i in range(count)]
    from_left = lax.ppermute(packed, "gz", ahead)
    if count == 2:
        return from_left
    from_right = lax.ppermute(packed, "gz", [(b, a) for a, b in ahead])
    lane = jnp.arange(LANES, dtype=jnp.int32)[None, :]
    return jnp.where(lane & 7 < WIDTH, from_left, from_right)


def spread_matrix(matrix, size):
    rows = VARIABLES * GROUP
    pick = lax.broadcasted_iota(jnp.int32, (rows, VARIABLES), 0) >> 4
    pick = (pick == lax.broadcasted_iota(jnp.int32, (rows, VARIABLES), 1)).astype(F32)
    tall = jnp.dot(pick, matrix, precision=lax.Precision.HIGHEST, preferred_element_type=F32)
    wide = lax.dot_general(
        tall, pick, (((1,), (1,)), ((), ())), precision=lax.Precision.HIGHEST, preferred_element_type=F32
    )
    row = lax.broadcasted_iota(jnp.int32, (rows, rows), 0) & (GROUP - 1)
    column = lax.broadcasted_iota(jnp.int32, (rows, rows), 1) & (GROUP - 1)
    return split(jnp.where(row == column, wide, 0.0))


def stencil(offset):
    size = jnp.abs(offset)
    weight = jnp.where(size == 1, 45.0, jnp.where(size == 2, -9.0, jnp.where(size == 3, 1.0, 0.0)))
    return jnp.where(offset < 0, -weight, weight)


def main_kernel(
    list_ref,
    count_ref,
    u_ref,
    face_ref,
    left_ref,
    right_ref,
    row_ref,
    out_ref,
    cells,
    pencils,
    turned,
    speed_t,
    press_t,
    g_out,
    g_in,
    delta,
    triple,
    smooth,
    curve,
    faces,
    change,
    edge,
    edge_t,
    slot_hot,
    speed_y,
    press_y,
    speed_z,
    press_z,
    flux_z,
    flux_y,
    band_y,
    band_z,
    band_h,
    picked_sem,
    in_sem,
    out_sem,
):
    _, cells_x, cells_y, cells_z = u_ref.shape
    slots = row_ref.shape[1]
    total = cells_x * cells_y
    span = turned.shape[1]
    def fetch(p, carry):
        place = list_ref[p]
        pltpu.make_async_copy(
            u_ref.at[:, place // cells_y, pl.ds(place % cells_y, 1), :], pencils.at[:, pl.ds(p, 1), :], picked_sem
        ).start()
        return carry

    lax.fori_loop(0, slots, fetch, 0)
    incoming = [
        pltpu.make_async_copy(u_ref.at[:, x], cells.at[:, pl.ds(x * cells_y, cells_y), :], in_sem.at[x])
        for x in range(cells_x)
    ]
    for copy in incoming:
        copy.start()

    left_high, left_low = spread_matrix(0.5 * left_ref[...], slots)
    right_high, right_low = spread_matrix(20.0 * right_ref[...], slots)
    live = count_ref[0]
    lane_slots = lax.broadcasted_iota(jnp.int32, (1, slots), 1)
    wanted = jnp.where(lane_slots < live, row_ref[...], -1)

    block_rows = band_y.shape[0]
    row = lax.broadcasted_iota(jnp.int32, (block_rows, block_rows), 0)
    column = lax.broadcasted_iota(jnp.int32, (block_rows, block_rows), 1)
    inside = row // cells_y == column // cells_y
    weights = jnp.where(inside, stencil(column - row), 0.0).astype(BF16)
    band_y[:, :block_rows] = weights
    band_y[:, block_rows:] = weights
    row = lax.broadcasted_iota(jnp.int32, (cells_z, cells_z), 0)
    column = lax.broadcasted_iota(jnp.int32, (cells_z, cells_z), 1)
    weights = stencil(row - column).astype(BF16)
    band_z[:cells_z, :] = weights
    band_z[cells_z:, :] = weights
    kind = lax.broadcasted_iota(jnp.int32, (LANES, cells_z), 0) & 7
    column = lax.broadcasted_iota(jnp.int32, (LANES, cells_z), 1)
    place = jnp.where(kind < WIDTH, kind - WIDTH, kind - WIDTH + cells_z)
    band_h[...] = jnp.where(kind < 2 * WIDTH, stencil(place - column), 0.0)

    for begin in range(0, total, LANES):
        edge_t[:, begin : begin + LANES] = face_ref[begin : begin + LANES, :].T
    fluxes = flux_of([edge_t[8 * v : 8 * v + 8, :] for v in range(VARIABLES)], 2)
    for v in range(VARIABLES):
        edge_t[8 * v : 8 * v + 8, :] = fluxes[v]
    for begin in range(0, total, LANES):
        pencil = begin + lax.broadcasted_iota(jnp.int32, (LANES, slots), 0)
        hot = (wanted == pencil).astype(F32)
        calm = 1.0 - jnp.sum(hot, axis=1, keepdims=True)
        hot = hot.astype(BF16)
        slot_hot[begin : begin + LANES, :slots] = hot
        slot_hot[begin : begin + LANES, slots:] = hot
        high, low = split(edge_t[:, begin : begin + LANES].T * calm)
        edge[begin : begin + LANES, :LANES] = high
        edge[begin : begin + LANES, LANES:] = low

    def neighbour(p, carry):
        speed_t[pl.ds(p, 1), :] = face_ref[pl.ds(list_ref[p], 1), :]
        return carry

    lax.fori_loop(0, slots, neighbour, 0, unroll=8)
    border = speed_t[0:slots, :].T

    pltpu.make_async_copy(pencils, pencils, picked_sem).wait()
    for v in range(VARIABLES):
        tile = border[8 * v : 8 * v + 8, :]
        turned[v, 0:LEAD, :] = tile
        turned[v, span - 8 : span, :] = tile
        turned[v, LEAD - WIDTH : LEAD - WIDTH + 8, :] = tile
        turned[v, LEAD + cells_z - WIDTH : LEAD + cells_z - WIDTH + 8, :] = tile
        for begin in range(0, cells_z, LANES):
            turned[v, LEAD + begin : LEAD + begin + LANES, :] = pencils[v, :, begin : begin + LANES].T

    top = jnp.zeros((8, slots), F32)
    for begin in range(0, span, 8):
        parts = [turned[v, begin : begin + 8, :] for v in range(VARIABLES)]
        inverse, pressure = state_of(parts)
        velocity = parts[SPECIES + 2] * inverse
        speed_t[begin : begin + 8, :] = velocity
        press_t[begin : begin + 8, :] = pressure
        size = jnp.abs(velocity)
        if begin < LEAD - WIDTH or begin + 8 > LEAD + cells_z + WIDTH:
            at = begin + lax.broadcasted_iota(jnp.int32, (8, slots), 0)
            size = jnp.where((at >= LEAD - WIDTH) & (at < LEAD + cells_z + WIDTH), size, 0.0)
        top = jnp.maximum(top, size)
    wave = 0.5 * (jnp.max(top, axis=0, keepdims=True) + 1.0)

    rows = VARIABLES * GROUP

    def project(index, carry):
        at = pl.ds(pl.multiple_of(index * GROUP, GROUP), GROUP)
        velocity = 0.5 * speed_t[at, :]
        pressure = 0.5 * press_t[at, :]
        parts = [turned[v, at, :] for v in range(VARIABLES)]
        flux = [part * velocity for part in parts]
        flux[SPECIES + 2] = flux[SPECIES + 2] + pressure
        flux[SPECIES + 3] = flux[SPECIES + 3] + 2.0 * pressure * velocity
        high, low = [], []
        for v in range(VARIABLES):
            one, two = split(jnp.concatenate([flux[v], wave * parts[v]], axis=1))
            high.append(one)
            low.append(two)
        high = jnp.concatenate(high, axis=0)
        low = jnp.concatenate(low, axis=0)
        both = dot(left_high, high) + dot(left_high, low) + dot(left_low, high)
        both = both.reshape(VARIABLES, GROUP, 2 * slots)
        g_out[:, at, :] = both[:, :, :slots] + both[:, :, slots:]
        g_in[:, at, :] = both[:, :, :slots] - both[:, :, slots:]
        return carry

    lax.fori_loop(0, span // GROUP, project, 0)

    def upwind(i, carry):
        for side, source in enumerate((g_out, g_in)):
            for begin in range(0, span, 8):
                step = source[i, begin + 1 : begin + 9, :] - source[i, begin : begin + 8, :]
                delta[side, begin : begin + 8, :] = step
                triple[side, begin : begin + 8, :] = 3.0 * step
            for begin in range(8, span, 8):
                bend = delta[side, begin : begin + 8, :] - delta[side, begin - 1 : begin + 7, :]
                curve[side, begin : begin + 8, :] = bend
                smooth[side, begin : begin + 8, :] = (13.0 / 3.0 * bend) * bend + weno_epsilon
            bend = delta[side, 1:9, :] - delta[side, 0:8, :]
            curve[side, 1:9, :] = bend
            smooth[side, 1:9, :] = (13.0 / 3.0 * bend) * bend + weno_epsilon
        for begin in range(0, cells_z + 8, 8):
            at = begin + LEAD - 1

            def read(ref, side, offset):
                return ref[side, at + offset : at + offset + 8, :]

            value = None
            for side, source, way in ((0, g_out, 1), (1, g_in, -1)):
                back = 0 if side == 0 else 1
                if side == 0:
                    d1, d2, d3, d4 = (read(delta, 0, o) for o in (-2, -1, 0, 1))
                    three2, three3 = read(triple, 0, -1), read(triple, 0, 0)
                    s1, s2, s3 = (read(smooth, 0, o) for o in (-1, 0, 1))
                    z1, z2, z3 = (read(curve, 0, o) for o in (-1, 0, 1))
                else:
                    d1, d2, d3, d4 = (read(delta, 1, o) for o in (2, 1, 0, -1))
                    three2, three3 = read(triple, 1, 1), read(triple, 1, 0)
                    s1, s2, s3 = (read(smooth, 1, o) for o in (2, 1, 0))
                    z1, z2, z3 = (read(curve, 1, o) for o in (2, 1, 0))
                centre = source[i, at + back : at + back + 8, :]
                t0 = three2 - d1
                t1 = d2 + d3
                t2 = d4 - three3
                r0 = pl.reciprocal(s1 + t0 * t0, approx=True)
                r1 = pl.reciprocal(s2 + t1 * t1, approx=True)
                r2 = pl.reciprocal(s3 + t2 * t2, approx=True)
                w0 = r0 * (r0 * (1.0 / 3.0))
                w1 = r1 * r1
                w2 = r2 * r2
                above = (w0 + w0) * (z2 - z1) + w2 * (z3 - z2)
                below = (w0 + w2) + (w1 + w1)
                bent = above * pl.reciprocal(below, approx=True)
                line = t1 + d3
                if side == 0:
                    value = 6.0 * centre + line - bent
                else:
                    value = value + (6.0 * centre - line - bent)
            faces[i, begin : begin + 8, :] = value
        return carry

    lax.fori_loop(0, VARIABLES, upwind, 0)

    keep = lane_slots < live

    def back(index, carry):
        base = pl.multiple_of(index * 2 * GROUP, 2 * GROUP)
        high, low = [], []
        for v in range(VARIABLES):
            pieces = []
            for begin in (0, GROUP):
                here = faces[v, pl.ds(base + begin, GROUP), :]
                after = faces[v, pl.ds(base + begin + 1, GROUP), :]
                pieces.append(after - here)
            one, two = split(jnp.concatenate(pieces, axis=1))
            high.append(one)
            low.append(two)
        high = jnp.concatenate(high, axis=0)
        low = jnp.concatenate(low, axis=0)
        both = dot(right_high, high) + dot(right_high, low) + dot(right_low, high)
        both = both.reshape(VARIABLES, GROUP, 2 * slots)
        for part, begin in enumerate((0, GROUP)):
            piece = jnp.where(keep[None], both[:, :, part * slots : part * slots + slots], 0.0)
            one, two = split(piece)
            change[:, pl.ds(base + begin, GROUP), :slots] = one
            change[:, pl.ds(base + begin, GROUP), slots:] = two
        return carry

    lax.fori_loop(0, cells_z // (2 * GROUP), back, 0)

    for copy in incoming:
        copy.wait()

    def state(index, carry):
        at = pl.ds(pl.multiple_of(index * 8, 8), 8)
        pencil = index * 8 + lax.broadcasted_iota(jnp.int32, (8, slots), 0)
        calm = 1.0 - jnp.sum((wanted == pencil).astype(F32), axis=1, keepdims=True)
        for begin in range(0, cells_z, LANES):
            wide = slice(begin, begin + LANES)
            parts = [cells[v, at, wide] for v in range(VARIABLES)]
            inverse, pressure = state_of(parts)
            speed_y[at, wide] = parts[SPECIES + 1] * inverse
            press_y[at, wide] = pressure
            speed_z[at, wide] = parts[SPECIES + 2] * inverse * calm
            press_z[at, wide] = pressure * calm
        return carry

    lax.fori_loop(0, total // 8, state, 0)

    blocks = total // block_rows

    def advance(block, carry):
        base = pl.multiple_of(block * block_rows, block_rows)
        for v in range(VARIABLES):
            turn = v % 2
            for begin in range(0, block_rows, 16):
                at = pl.ds(base + begin, 16)
                value = cells[v, at, :]
                along_y = value * speed_y[at, :]
                along_z = value * speed_z[at, :]
                if v == SPECIES + 1:
                    along_y = along_y + press_y[at, :]
                if v == SPECIES + 2:
                    along_z = along_z + press_z[at, :]
                if v == SPECIES + 3:
                    along_y = along_y + press_y[at, :] * speed_y[at, :]
                    along_z = along_z + press_y[at, :] * speed_z[at, :]
                high, low = split(along_y)
                flux_y[turn, begin : begin + 16, :] = high
                flux_y[turn, block_rows + begin : block_rows + begin + 16, :] = low
                high, low = split(along_z)
                flux_z[turn, begin : begin + 16, :cells_z] = high
                flux_z[turn, begin : begin + 16, cells_z:] = low
            lanes = lax.broadcasted_iota(jnp.int32, (LANES, cells_z), 0) >> 3
            own = jnp.where(lanes == v, band_h[...], 0.0).astype(BF16)
            at = pl.ds(base, block_rows)
            gained = dot(flux_z[turn], band_z[...])
            gained = gained + dot(band_y[...], flux_y[turn])
            gained = gained + lax.dot_general(
                slot_hot[at, :], change[v], (((1,), (1,)), ((), ())), preferred_element_type=F32
            )
            gained = gained + dot(edge[at, :], jnp.concatenate([own, own], axis=0))
            cells[v, at, :] = cells[v, at, :] - (time_step / 60.0) * gained
        for x in range(block_rows // cells_y):
            pltpu.make_async_copy(
                cells.at[:, pl.ds(base + x * cells_y, cells_y), :],
                out_ref.at[:, block * (block_rows // cells_y) + x],
                out_sem,
            ).start()
        return carry

    lax.fori_loop(0, blocks, advance, 0)
    pltpu.make_async_copy(cells, cells, out_sem).wait()


def main(listed, count, conserved, face, char_left, char_right):
    _, cells_x, cells_y, cells_z = conserved.shape
    slots = listed.shape[0]
    total = cells_x * cells_y
    span = -(-(cells_z + 2 * LEAD) // GROUP) * GROUP
    block_rows = cells_y * max(1, min(cells_x, 256 // cells_y))
    vmem = pltpu.VMEM
    scratch = [
        vmem((VARIABLES, total, cells_z), F32),
        vmem((VARIABLES, slots, cells_z), F32),
        vmem((VARIABLES, span, slots), F32),
        vmem((span, slots), F32),
        vmem((span, slots), F32),
        vmem((VARIABLES, span + 8, slots), F32),
        vmem((VARIABLES, span + 8, slots), F32),
        vmem((2, span + 8, slots), F32),
        vmem((2, span + 8, slots), F32),
        vmem((2, span + 8, slots), F32),
        vmem((2, span + 8, slots), F32),
        vmem((VARIABLES, cells_z + 8, slots), F32),
        vmem((VARIABLES, cells_z, 2 * slots), BF16),
        vmem((total, 2 * LANES), BF16),
        vmem((LANES, total), F32),
        vmem((total, 2 * slots), BF16),
        vmem((total, cells_z), F32),
        vmem((total, cells_z), F32),
        vmem((total, cells_z), F32),
        vmem((total, cells_z), F32),
        vmem((2, block_rows, 2 * cells_z), BF16),
        vmem((2, 2 * block_rows, cells_z), BF16),
        vmem((block_rows, 2 * block_rows), BF16),
        vmem((2 * cells_z, cells_z), BF16),
        vmem((LANES, cells_z), F32),
        pltpu.SemaphoreType.DMA(()),
        pltpu.SemaphoreType.DMA((cells_x,)),
        pltpu.SemaphoreType.DMA(()),
    ]
    smem = pl.BlockSpec(memory_space=pltpu.SMEM)
    whole = pl.BlockSpec(memory_space=pltpu.VMEM)
    anywhere = pl.BlockSpec(memory_space=pl.ANY)
    return pl.pallas_call(
        main_kernel,
        out_shape=jax.ShapeDtypeStruct(conserved.shape, F32),
        in_specs=[smem, smem, anywhere, whole, whole, whole, whole],
        out_specs=anywhere,
        scratch_shapes=scratch,
        compiler_params=pltpu.CompilerParams(vmem_limit_bytes=56 << 20),
        cost_estimate=pl.CostEstimate(flops=8_000_000_000, bytes_accessed=16_000_000, transcendentals=4_000_000),
        name="section",
    )(listed, count, conserved, face, char_left, char_right, listed.reshape(1, slots))


def edge_kernel(out_in, before_ref, after_ref, out_ref, low_rows, high_rows, in_sem, out_sem):
    cells_x, cells_y = out_in.shape[1], out_in.shape[2]
    for x in range(cells_x):
        for j in range(WIDTH):
            pltpu.make_async_copy(
                out_in.at[:, x, pl.ds(j, 1), :], low_rows.at[j, :, pl.ds(x, 1), :], in_sem
            ).start()
            pltpu.make_async_copy(
                out_in.at[:, x, pl.ds(cells_y - WIDTH + j, 1), :], high_rows.at[j, :, pl.ds(x, 1), :], in_sem
            ).start()
    pltpu.make_async_copy(low_rows, low_rows, in_sem).wait()
    pltpu.make_async_copy(high_rows, high_rows, in_sem).wait()
    scale = time_step / 60.0
    for begin in range(0, out_in.shape[3], LANES):
        wide = slice(begin, begin + LANES)
        f0, f1, f2 = (flux_of([before_ref[j, v, :, wide] for v in range(VARIABLES)], 1) for j in range(WIDTH))
        for v in range(VARIABLES):
            low_rows[0, v, :, wide] += scale * (45.0 * f2[v] - 9.0 * f1[v] + f0[v])
            low_rows[1, v, :, wide] += scale * (f1[v] - 9.0 * f2[v])
            low_rows[2, v, :, wide] += scale * f2[v]
        f0, f1, f2 = (flux_of([after_ref[j, v, :, wide] for v in range(VARIABLES)], 1) for j in range(WIDTH))
        for v in range(VARIABLES):
            high_rows[2, v, :, wide] -= scale * (45.0 * f0[v] - 9.0 * f1[v] + f2[v])
            high_rows[1, v, :, wide] -= scale * (f1[v] - 9.0 * f0[v])
            high_rows[0, v, :, wide] -= scale * f0[v]
    for x in range(cells_x):
        for j in range(WIDTH):
            pltpu.make_async_copy(
                low_rows.at[j, :, pl.ds(x, 1), :], out_ref.at[:, x, pl.ds(j, 1), :], out_sem
            ).start()
            pltpu.make_async_copy(
                high_rows.at[j, :, pl.ds(x, 1), :], out_ref.at[:, x, pl.ds(cells_y - WIDTH + j, 1), :], out_sem
            ).start()
    pltpu.make_async_copy(low_rows, low_rows, out_sem).wait()
    pltpu.make_async_copy(high_rows, high_rows, out_sem).wait()


def add_edges(advanced, before, after):
    anywhere = pl.BlockSpec(memory_space=pl.ANY)
    whole = pl.BlockSpec(memory_space=pltpu.VMEM)
    return pl.pallas_call(
        edge_kernel,
        out_shape=jax.ShapeDtypeStruct(advanced.shape, F32),
        in_specs=[anywhere, whole, whole],
        out_specs=anywhere,
        scratch_shapes=[
            pltpu.VMEM(before.shape, F32),
            pltpu.VMEM(before.shape, F32),
            pltpu.SemaphoreType.DMA(()),
            pltpu.SemaphoreType.DMA(()),
        ],
        input_output_aliases={0: 0},
        cost_estimate=pl.CostEstimate(flops=5_000_000, bytes_accessed=2_000_000, transcendentals=0),
        name="edges",
    )(advanced, before, after)


def on_device(conserved, char_left, char_right, shock_list, shock_count):
    slots = shock_list.shape[-1]
    count = lax.axis_size("gy")
    ahead = [(i, (i + 1) % count) for i in range(count)]
    tail, head = pack_y(conserved)
    before = lax.ppermute(tail, "gy", ahead)
    after = lax.ppermute(head, "gy", [(b, a) for a, b in ahead])
    face = exchange_z(pack_z(conserved))
    advanced = main(
        shock_list.reshape(slots), shock_count.reshape(1), conserved, face, char_left, char_right
    )
    return add_edges(advanced, before, after)


def solution(mesh):
    placed = (P(None, "gx", "gy", "gz"), P(), P(), P("gx", "gy", "gz", None), P("gx", "gy", "gz"))
    return jax.shard_map(
        on_device, mesh=mesh, in_specs=placed, out_specs=P(None, "gx", "gy", "gz"), check_vma=False
    )
```

```python
import functools

import jax
import jax.numpy as jnp
from jax import lax
from jax.experimental import pallas as pl
from jax.experimental.pallas import tpu as pltpu
from jax.sharding import PartitionSpec as P

SPECIES = 9
VARIABLES = 14
WIDTH = 3
GROUP = 16
LANES = 128
LEAD = 8

gas_excess = 0.4
time_step = 0.2
weno_epsilon = 1e-06

F32 = jnp.float32
BF16 = jnp.bfloat16


def split(values):
    high = values.astype(BF16)
    low = (values - high.astype(F32)).astype(BF16)
    return high, low


def dot(left, right):
    return jnp.dot(left, right, preferred_element_type=F32)


def state_of(parts):
    density = parts[0]
    for index in range(1, SPECIES):
        density = density + parts[index]
    inverse = pl.reciprocal(density, approx=True)
    first, second, last = parts[SPECIES], parts[SPECIES + 1], parts[SPECIES + 2]
    kinetic = 0.5 * (first * first + second * second + last * last) * inverse
    pressure = gas_excess * (parts[SPECIES + 3] - parts[SPECIES + 4] - kinetic)
    return inverse, pressure


def flux_of(parts, normal):
    inverse, pressure = state_of(parts)
    velocity = parts[SPECIES + normal] * inverse
    result = [part * velocity for part in parts]
    result[SPECIES + normal] = result[SPECIES + normal] + pressure
    result[SPECIES + 3] = result[SPECIES + 3] + pressure * velocity
    return result


def pack_y_kernel(u_ref, tail_ref, head_ref, sem):
    cells_x, cells_y = u_ref.shape[1], u_ref.shape[2]
    for x in range(cells_x):
        for j in range(WIDTH):
            pltpu.make_async_copy(
                u_ref.at[:, x, pl.ds(cells_y - WIDTH + j, 1), :], tail_ref.at[j, :, pl.ds(x, 1), :], sem
            ).start()
            pltpu.make_async_copy(
                u_ref.at[:, x, pl.ds(j, 1), :], head_ref.at[j, :, pl.ds(x, 1), :], sem
            ).start()
    pltpu.make_async_copy(tail_ref, tail_ref, sem).wait()
    pltpu.make_async_copy(head_ref, head_ref, sem).wait()


def pack_y(conserved):
    cells_x, cells_z = conserved.shape[1], conserved.shape[3]
    face = jax.ShapeDtypeStruct((WIDTH, VARIABLES, cells_x, cells_z), F32)
    return pl.pallas_call(
        pack_y_kernel,
        out_shape=[face, face],
        in_specs=[pl.BlockSpec(memory_space=pl.ANY)],
        out_specs=[pl.BlockSpec(memory_space=pltpu.VMEM)] * 2,
        scratch_shapes=[pltpu.SemaphoreType.DMA(())],
        cost_estimate=pl.CostEstimate(flops=0, bytes_accessed=2_000_000, transcendentals=0),
        name="pack_y",
    )(conserved)


def pack_z_kernel(u_ref, out_ref):
    cells_z = u_ref.shape[3]
    lane = lax.broadcasted_iota(jnp.int32, (u_ref.shape[2], LANES), 1)
    packed = jnp.zeros((u_ref.shape[2], LANES), F32)
    for v in range(VARIABLES):
        both = jnp.where(lane < LANES // 2, u_ref[v, 0, :, :LANES], u_ref[v, 0, :, cells_z - LANES :])
        packed = jnp.where(lane >> 3 == v, pltpu.roll(both, 8 * v + WIDTH, 1), packed)
    out_ref[...] = packed


def pack_z(conserved):
    _, cells_x, cells_y, cells_z = conserved.shape
    return pl.pallas_call(
        pack_z_kernel,
        out_shape=jax.ShapeDtypeStruct((cells_x * cells_y, LANES), F32),
        grid=(cells_x,),
        in_specs=[pl.BlockSpec((VARIABLES, 1, cells_y, cells_z), lambda x: (0, x, 0, 0))],
        out_specs=pl.BlockSpec((cells_y, LANES), lambda x: (x, 0)),
        compiler_params=pltpu.CompilerParams(vmem_limit_bytes=60 << 20),
        cost_estimate=pl.CostEstimate(flops=4_000_000, bytes_accessed=7_600_000, transcendentals=0),
        name="pack_z",
    )(conserved)


def exchange_z(packed):
    count = lax.axis_size("gz")
    if count == 1:
        return packed
    ahead = [(i, (i + 1) % count) for i in range(count)]
    from_left = lax.ppermute(packed, "gz", ahead)
    if count == 2:
        return from_left
    from_right = lax.ppermute(packed, "gz", [(b, a) for a, b in ahead])
    lane = jnp.arange(LANES, dtype=jnp.int32)[None, :]
    return jnp.where(lane & 7 < WIDTH, from_left, from_right)


def spread_matrix(matrix):
    rows = VARIABLES * GROUP
    pick = lax.broadcasted_iota(jnp.int32, (rows, VARIABLES), 0) >> 4
    pick = (pick == lax.broadcasted_iota(jnp.int32, (rows, VARIABLES), 1)).astype(F32)
    tall = jnp.dot(pick, matrix, precision=lax.Precision.HIGHEST, preferred_element_type=F32)
    wide = lax.dot_general(
        tall, pick, (((1,), (1,)), ((), ())), precision=lax.Precision.HIGHEST, preferred_element_type=F32
    )
    row = lax.broadcasted_iota(jnp.int32, (rows, rows), 0) & (GROUP - 1)
    column = lax.broadcasted_iota(jnp.int32, (rows, rows), 1) & (GROUP - 1)
    return split(jnp.where(row == column, wide, 0.0))


def stencil(offset):
    size = jnp.abs(offset)
    weight = jnp.where(size == 1, 45.0, jnp.where(size == 2, -9.0, jnp.where(size == 3, 1.0, 0.0)))
    return jnp.where(offset < 0, -weight, weight)


def shock_kernel(
    list_ref,
    count_ref,
    u_ref,
    face_ref,
    left_ref,
    right_ref,
    row_ref,
    change_ref,
    hot_ref,
    edge_ref,
    state_ref,
    cells,
    pencils,
    turned,
    speed_t,
    press_t,
    g_out,
    g_in,
    delta,
    triple,
    smooth,
    curve,
    third,
    faces,
    edge_t,
    near,
    picked_sem,
    in_sem,
    near_sem,
):
    _, cells_x, cells_y, cells_z = u_ref.shape
    slots = row_ref.shape[1]
    total = cells_x * cells_y
    span = turned.shape[1]
    nearby = pltpu.make_async_copy(face_ref, near, near_sem)
    nearby.start()

    def fetch(p, carry):
        place = list_ref[p]
        pltpu.make_async_copy(
            u_ref.at[:, place // cells_y, pl.ds(place % cells_y, 1), :], pencils.at[:, pl.ds(p, 1), :], picked_sem
        ).start()
        return carry

    lax.fori_loop(0, slots, fetch, 0)
    incoming = [
        pltpu.make_async_copy(u_ref.at[:, x], cells.at[:, pl.ds(x * cells_y, cells_y), :], in_sem.at[x])
        for x in range(cells_x)
    ]
    for copy in incoming:
        copy.start()

    left_high, left_low = spread_matrix(0.5 * left_ref[...])
    right_high, right_low = spread_matrix((time_step / 3.0) * right_ref[...])
    live = count_ref[0]
    lane_slots = lax.broadcasted_iota(jnp.int32, (1, slots), 1)
    wanted = jnp.where(lane_slots < live, row_ref[...], -1)
    scale = time_step / 60.0

    nearby.wait()
    for begin in range(0, total, LANES):
        edge_t[:, begin : begin + LANES] = near[begin : begin + LANES, :].T
    fluxes = flux_of([edge_t[8 * v : 8 * v + 8, :] for v in range(VARIABLES)], 2)
    for v in range(VARIABLES):
        edge_t[8 * v : 8 * v + 8, :] = fluxes[v]
    row = lax.broadcasted_iota(jnp.int32, (LANES, LANES), 0)
    column = lax.broadcasted_iota(jnp.int32, (LANES, LANES), 1)
    target, source = row & 7, column & 7
    reach = jnp.logical_xor(target < WIDTH, source < WIDTH)
    reach = reach & (target < 2 * WIDTH) & (source < 2 * WIDTH) & (row >> 3 == column >> 3)
    weights = jnp.where(reach, stencil(source - target), 0.0).astype(BF16)
    for begin in range(0, total, LANES):
        wide = slice(begin, begin + LANES)
        high, low = split(edge_t[:, wide])
        pencil = begin + lax.broadcasted_iota(jnp.int32, (LANES, slots), 0)
        hot = (wanted == pencil).astype(F32)
        calm = scale - scale * jnp.sum(hot, axis=1, keepdims=True)
        edge_ref[wide, :] = (dot(weights, high) + dot(weights, low)).T * calm
        hot = hot.astype(BF16)
        hot_ref[wide, :slots] = hot
        hot_ref[wide, slots:] = hot

    def neighbour(p, carry):
        speed_t[pl.ds(p, 1), :] = near[pl.ds(list_ref[p], 1), :]
        return carry

    lax.fori_loop(0, slots, neighbour, 0, unroll=8)
    border = speed_t[0:slots, :].T

    def state(index, carry):
        at = pl.ds(pl.multiple_of(index * 8, 8), 8)
        pencil = index * 8 + lax.broadcasted_iota(jnp.int32, (8, slots), 0)
        calm = scale - scale * jnp.sum((wanted == pencil).astype(F32), axis=1, keepdims=True)
        for begin in range(0, cells_z, LANES):
            wide = slice(begin, begin + LANES)
            parts = [cells[v, at, wide] for v in range(VARIABLES)]
            inverse, pressure = state_of(parts)
            state_ref[0, at, wide] = parts[SPECIES + 1] * (inverse * scale)
            state_ref[1, at, wide] = parts[SPECIES + 2] * (inverse * calm)
            state_ref[2, at, wide] = pressure
            state_ref[3, at, wide] = pressure * calm
        return carry

    for x in range(cells_x):
        incoming[x].wait()
        lax.fori_loop(x * cells_y // 8, (x + 1) * cells_y // 8, state, 0, unroll=True)

    pltpu.make_async_copy(pencils, pencils, picked_sem).wait()
    for v in range(VARIABLES):
        tile = border[8 * v : 8 * v + 8, :]
        turned[v, 0:LEAD, :] = tile
        turned[v, span - 8 : span, :] = tile
        turned[v, LEAD - WIDTH : LEAD - WIDTH + 8, :] = tile
        turned[v, LEAD + cells_z - WIDTH : LEAD + cells_z - WIDTH + 8, :] = tile
        for begin in range(0, cells_z, LANES):
            turned[v, LEAD + begin : LEAD + begin + LANES, :] = pencils[v, :, begin : begin + LANES].T

    top = jnp.zeros((8, slots), F32)
    for begin in range(0, span, 8):
        parts = [turned[v, begin : begin + 8, :] for v in range(VARIABLES)]
        inverse, pressure = state_of(parts)
        velocity = parts[SPECIES + 2] * inverse
        speed_t[begin : begin + 8, :] = 0.5 * velocity
        press_t[begin : begin + 8, :] = pressure
        size = jnp.abs(velocity)
        if begin < LEAD - WIDTH or begin + 8 > LEAD + cells_z + WIDTH:
            at = begin + lax.broadcasted_iota(jnp.int32, (8, slots), 0)
            size = jnp.where((at >= LEAD - WIDTH) & (at < LEAD + cells_z + WIDTH), size, 0.0)
        top = jnp.maximum(top, size)
    wave = 0.5 * (jnp.max(top, axis=0, keepdims=True) + 1.0)

    def project(index, carry):
        at = pl.ds(pl.multiple_of(index * GROUP, GROUP), GROUP)
        velocity = speed_t[at, :]
        pressure = press_t[at, :]
        parts = [turned[v, at, :] for v in range(VARIABLES)]
        flux = [part * velocity for part in parts]
        flux[SPECIES + 2] = flux[SPECIES + 2] + 0.5 * pressure
        flux[SPECIES + 3] = flux[SPECIES + 3] + pressure * velocity
        high, low = [], []
        for v in range(VARIABLES):
            one, two = split(jnp.concatenate([flux[v], wave * parts[v]], axis=1))
            high.append(one)
            low.append(two)
        high = jnp.concatenate(high, axis=0)
        low = jnp.concatenate(low, axis=0)
        both = dot(left_high, high) + dot(left_high, low) + dot(left_low, high)
        both = both.reshape(VARIABLES, GROUP, 2 * slots)
        g_out[:, at, :] = both[:, :, :slots] + both[:, :, slots:]
        g_in[:, at, :] = both[:, :, :slots] - both[:, :, slots:]
        return carry

    lax.fori_loop(0, span // GROUP, project, 0, unroll=True)

    def upwind(i, carry):
        for side, source in enumerate((g_out, g_in)):
            for begin in range(0, span, 8):
                step = source[i, begin + 1 : begin + 9, :] - source[i, begin : begin + 8, :]
                delta[side, begin : begin + 8, :] = step
                triple[side, begin : begin + 8, :] = 3.0 * step
            for begin in range(1, span, 8):
                bend = delta[side, begin : begin + 8, :] - delta[side, begin - 1 : begin + 7, :]
                curve[side, begin : begin + 8, :] = bend
                smooth[side, begin : begin + 8, :] = (13.0 / 3.0 * bend) * bend + weno_epsilon
            for begin in range(0, span, 8):
                third[side, begin : begin + 8, :] = (
                    curve[side, begin + 1 : begin + 9, :] - curve[side, begin : begin + 8, :]
                )
        for begin in range(0, cells_z + 8, 8):
            at = begin + LEAD - 1

            def read(ref, side, offset):
                return ref[side, at + offset : at + offset + 8, :]

            value = None
            for side, source in enumerate((g_out, g_in)):
                if side == 0:
                    d1, d2, d3, d4 = (read(delta, 0, o) for o in (-2, -1, 0, 1))
                    three2, three3 = read(triple, 0, -1), read(triple, 0, 0)
                    s1, s2, s3 = (read(smooth, 0, o) for o in (-1, 0, 1))
                    u1, u2 = (read(third, 0, o) for o in (-1, 0))
                else:
                    d1, d2, d3, d4 = (read(delta, 1, o) for o in (2, 1, 0, -1))
                    three2, three3 = read(triple, 1, 1), read(triple, 1, 0)
                    s1, s2, s3 = (read(smooth, 1, o) for o in (2, 1, 0))
                    u1, u2 = (read(third, 1, o) for o in (1, 0))
                centre = source[i, at + side : at + side + 8, :]
                t0 = three2 - d1
                t1 = d2 + d3
                t2 = d4 - three3
                r0 = pl.reciprocal(s1 + t0 * t0, approx=True)
                r1 = pl.reciprocal(s2 + t1 * t1, approx=True)
                r2 = pl.reciprocal(s3 + t2 * t2, approx=True)
                w0 = r0 * (r0 * (1.0 / 3.0))
                w1 = r1 * r1
                w2 = r2 * r2
                above = (w0 + w0) * u1 + w2 * u2
                below = (w0 + w2) + (w1 + w1)
                bent = above * pl.reciprocal(below, approx=True)
                line = t1 + d3
                if side == 0:
                    value = 6.0 * centre + line - bent
                else:
                    value = value + (6.0 * centre - line + bent)
            faces[i, begin : begin + 8, :] = value
        return carry

    lax.fori_loop(0, VARIABLES, upwind, 0)

    keep = lane_slots < live

    def back(index, carry):
        base = pl.multiple_of(index * 2 * GROUP, 2 * GROUP)
        high, low = [], []
        for v in range(VARIABLES):
            pieces = []
            for begin in (0, GROUP):
                here = faces[v, pl.ds(base + begin, GROUP), :]
                after = faces[v, pl.ds(base + begin + 1, GROUP), :]
                pieces.append(after - here)
            one, two = split(jnp.concatenate(pieces, axis=1))
            high.append(one)
            low.append(two)
        high = jnp.concatenate(high, axis=0)
        low = jnp.concatenate(low, axis=0)
        both = dot(right_high, high) + dot(right_high, low) + dot(right_low, high)
        both = both.reshape(VARIABLES, GROUP, 2 * slots)
        for part, begin in enumerate((0, GROUP)):
            piece = jnp.where(keep[None], both[:, :, part * slots : part * slots + slots], 0.0)
            one, two = split(piece)
            change_ref[:, pl.ds(base + begin, GROUP), :slots] = one
            change_ref[:, pl.ds(base + begin, GROUP), slots:] = two
        return carry

    lax.fori_loop(0, cells_z // (2 * GROUP), back, 0, unroll=True)


def shock(listed, count, conserved, face, char_left, char_right):
    _, cells_x, cells_y, cells_z = conserved.shape
    slots = listed.shape[0]
    total = cells_x * cells_y
    span = -(-(cells_z + 2 * LEAD) // GROUP) * GROUP
    vmem = pltpu.VMEM
    work = vmem((2, span + 8, slots), F32)
    scratch = [
        vmem((VARIABLES, total, cells_z), F32),
        vmem((VARIABLES, slots, cells_z), F32),
        vmem((VARIABLES, span, slots), F32),
        vmem((span, slots), F32),
        vmem((span, slots), F32),
        vmem((VARIABLES, span + 8, slots), F32),
        vmem((VARIABLES, span + 8, slots), F32),
        work,
        work,
        work,
        work,
        work,
        vmem((VARIABLES, cells_z + 8, slots), F32),
        vmem((LANES, total), F32),
        vmem((total, LANES), F32),
        pltpu.SemaphoreType.DMA(()),
        pltpu.SemaphoreType.DMA((cells_x,)),
        pltpu.SemaphoreType.DMA(()),
    ]
    smem = pl.BlockSpec(memory_space=pltpu.SMEM)
    whole = pl.BlockSpec(memory_space=pltpu.VMEM)
    anywhere = pl.BlockSpec(memory_space=pl.ANY)
    return pl.pallas_call(
        shock_kernel,
        out_shape=[
            jax.ShapeDtypeStruct((VARIABLES, cells_z, 2 * slots), BF16),
            jax.ShapeDtypeStruct((total, 2 * slots), BF16),
            jax.ShapeDtypeStruct((total, LANES), F32),
            jax.ShapeDtypeStruct((4, total, cells_z), F32),
        ],
        in_specs=[smem, smem, anywhere, anywhere, whole, whole, whole],
        out_specs=[whole] * 4,
        scratch_shapes=scratch,
        compiler_params=pltpu.CompilerParams(vmem_limit_bytes=48 << 20),
        cost_estimate=pl.CostEstimate(flops=6_000_000_000, bytes_accessed=14_000_000, transcendentals=4_000_000),
        name="shock",
    )(listed, count, conserved, face, char_left, char_right, listed.reshape(1, slots))


def advance_kernel(
    u_ref, change_ref, hot_ref, edge_ref, state_ref, before_ref, after_ref, out_ref, fluxes, along_y, around, band
):
    total, cells_z = u_ref.shape[1], u_ref.shape[2]
    cells_x = before_ref.shape[2]
    cells_y = total // cells_x
    pitch = cells_y + 16
    v = pl.program_id(0)
    scale = time_step / 60.0
    normal_y = v == SPECIES + 1
    normal_z = v == SPECIES + 2
    energy = v == SPECIES + 3

    @pl.when(v == 0)
    def _():
        row = lax.broadcasted_iota(jnp.int32, (cells_z, cells_z), 0)
        column = lax.broadcasted_iota(jnp.int32, (cells_z, cells_z), 1)
        weights = stencil(row - column).astype(BF16)
        band[:cells_z, :] = weights
        band[cells_z:, :] = weights
        for side, source in enumerate((before_ref, after_ref)):
            for j in range(WIDTH):
                for begin in range(0, cells_z, LANES):
                    wide = slice(begin, begin + LANES)
                    parts = [source[j, i, :, wide] for i in range(VARIABLES)]
                    inverse, pressure = state_of(parts)
                    around[side, j, 0, :, wide] = parts[SPECIES + 1] * (inverse * scale)
                    around[side, j, 1, :, wide] = pressure

    def fill(extra_y, extra_z):
        for side, source in enumerate((before_ref, after_ref)):
            for j in range(WIDTH):
                for half in range(cells_z // LANES):
                    wide = slice(half * LANES, half * LANES + LANES)
                    value = source[j, v, :, wide]
                    value = extra_y(value, around[side, j, 0, :, wide], around[side, j, 1, :, wide])
                    begin = 8 - WIDTH + j if side == 0 else 8 + cells_y + j
                    along_y[half, pl.ds(begin, cells_x, stride=pitch), :] = value
        for begin in range(0, total, GROUP):
            at = slice(begin, begin + GROUP)
            place = begin // cells_y * pitch + 8 + begin % cells_y
            for half in range(cells_z // LANES):
                wide = slice(half * LANES, half * LANES + LANES)
                value = u_ref[0, at, wide]
                along_y[half, place : place + GROUP, :] = extra_y(value, state_ref[0, at, wide], state_ref[2, at, wide])
                high, low = split(extra_z(value, state_ref[1, at, wide], at, wide))
                fluxes[at, half * LANES : half * LANES + LANES] = high
                fluxes[at, cells_z + half * LANES : cells_z + half * LANES + LANES] = low

    plain_y = lambda value, speed, pressure: value * speed
    plain_z = lambda value, speed, at, wide: value * speed

    @pl.when(jnp.logical_not(normal_y | normal_z | energy))
    def _():
        fill(plain_y, plain_z)

    @pl.when(normal_y)
    def _():
        fill(lambda value, speed, pressure: value * speed + scale * pressure, plain_z)

    @pl.when(normal_z)
    def _():
        fill(plain_y, lambda value, speed, at, wide: value * speed + state_ref[3, at, wide])

    @pl.when(energy)
    def _():
        fill(
            lambda value, speed, pressure: (value + pressure) * speed,
            lambda value, speed, at, wide: (value + state_ref[2, at, wide]) * speed,
        )

    lane = lax.broadcasted_iota(jnp.int32, (GROUP, LANES), 1)
    turn = (LANES - WIDTH - 8 * v) & (LANES - 1)
    rows = min(total, 256)
    for base in range(0, total, rows):
        gained = dot(fluxes[base : base + rows, :], band[...])
        gained = gained + lax.dot_general(
            hot_ref[base : base + rows, :], change_ref[0], (((1,), (1,)), ((), ())), preferred_element_type=F32
        )
        for begin in range(base, base + rows, GROUP):
            at = slice(begin, begin + GROUP)
            place = begin // cells_y * pitch + 8 + begin % cells_y
            border = pltpu.roll(edge_ref[at, :], turn, 1)
            for half in range(cells_z // LANES):
                wide = slice(half * LANES, half * LANES + LANES)

                def read(offset):
                    return along_y[half, place + offset : place + offset + GROUP, :]

                value = u_ref[0, at, wide] - gained[begin - base : begin - base + GROUP, wide]
                value = value - (
                    45.0 * (read(1) - read(-1)) - 9.0 * (read(2) - read(-2)) + (read(3) - read(-3))
                )
                if half == 0:
                    value = value - jnp.where(lane < WIDTH, border, 0.0)
                if half == cells_z // LANES - 1:
                    value = value - jnp.where(lane >= LANES - WIDTH, border, 0.0)
                out_ref[0, at, wide] = value


def advance(conserved, change, hot, edge, state, before, after):
    _, cells_x, cells_y, cells_z = conserved.shape
    total = cells_x * cells_y
    one = pl.BlockSpec((1, total, cells_z), lambda v: (v, 0, 0))

    def fixed(array):
        return pl.BlockSpec(array.shape, lambda v: (0,) * array.ndim)

    result = pl.pallas_call(
        advance_kernel,
        out_shape=jax.ShapeDtypeStruct((VARIABLES, total, cells_z), F32),
        grid=(VARIABLES,),
        in_specs=[
            one,
            pl.BlockSpec((1,) + change.shape[1:], lambda v: (v, 0, 0)),
            fixed(hot),
            fixed(edge),
            fixed(state),
            fixed(before),
            fixed(after),
        ],
        out_specs=one,
        scratch_shapes=[
            pltpu.VMEM((total, 2 * cells_z), BF16),
            pltpu.VMEM((cells_z // LANES, cells_x * (cells_y + 16), LANES), F32),
            pltpu.VMEM((2, WIDTH, 2, cells_x, cells_z), F32),
            pltpu.VMEM((2 * cells_z, cells_z), BF16),
        ],
        compiler_params=pltpu.CompilerParams(vmem_limit_bytes=24 << 20),
        cost_estimate=pl.CostEstimate(flops=4_000_000_000, bytes_accessed=20_000_000, transcendentals=0),
        name="advance",
    )(conserved.reshape(VARIABLES, total, cells_z), change, hot, edge, state, before, after)
    return result.reshape(conserved.shape)


def on_device(conserved, char_left, char_right, shock_list, shock_count):
    slots = shock_list.shape[-1]
    count = lax.axis_size("gy")
    ahead = [(i, (i + 1) % count) for i in range(count)]
    tail, head = pack_y(conserved)
    before = lax.ppermute(tail, "gy", ahead)
    after = lax.ppermute(head, "gy", [(b, a) for a, b in ahead])
    face = exchange_z(pack_z(conserved))
    change, hot, edge, state = shock(
        shock_list.reshape(slots), shock_count.reshape(1), conserved, face, char_left, char_right
    )
    return advance(conserved, change, hot, edge, state, before, after)


def solution(mesh):
    placed = (P(None, "gx", "gy", "gz"), P(), P(), P("gx", "gy", "gz", None), P("gx", "gy", "gz"))
    return jax.shard_map(
        on_device, mesh=mesh, in_specs=placed, out_specs=P(None, "gx", "gy", "gz"), check_vma=False
    )
```

```python
import functools

import jax
import jax.numpy as jnp
from jax import lax
from jax.experimental import pallas as pl
from jax.experimental.pallas import tpu as pltpu
from jax.sharding import PartitionSpec as P

SPECIES = 9
VARIABLES = 14
WIDTH = 3
GROUP = 16
LANES = 128
LEAD = 8

gas_excess = 0.4
time_step = 0.2
weno_epsilon = 1e-06

F32 = jnp.float32
BF16 = jnp.bfloat16


def split(values):
    high = values.astype(BF16)
    low = (values - high.astype(F32)).astype(BF16)
    return high, low


def dot(left, right):
    return jnp.dot(left, right, preferred_element_type=F32)


def state_of(parts):
    density = parts[0]
    for index in range(1, SPECIES):
        density = density + parts[index]
    inverse = pl.reciprocal(density, approx=True)
    first, second, last = parts[SPECIES], parts[SPECIES + 1], parts[SPECIES + 2]
    kinetic = 0.5 * (first * first + second * second + last * last) * inverse
    pressure = gas_excess * (parts[SPECIES + 3] - parts[SPECIES + 4] - kinetic)
    return inverse, pressure


def flux_of(parts, normal):
    inverse, pressure = state_of(parts)
    velocity = parts[SPECIES + normal] * inverse
    result = [part * velocity for part in parts]
    result[SPECIES + normal] = result[SPECIES + normal] + pressure
    result[SPECIES + 3] = result[SPECIES + 3] + pressure * velocity
    return result


def pack_kernel(u_ref, tail_ref, head_ref, face_ref, row_sem):
    _, cells_x, cells_y, cells_z = u_ref.shape
    for x in range(cells_x):
        for j in range(WIDTH):
            pltpu.make_async_copy(
                u_ref.at[:, x, pl.ds(cells_y - WIDTH + j, 1), :], tail_ref.at[j, :, pl.ds(x, 1), :], row_sem
            ).start()
            pltpu.make_async_copy(
                u_ref.at[:, x, pl.ds(j, 1), :], head_ref.at[j, :, pl.ds(x, 1), :], row_sem
            ).start()
    lane = lax.broadcasted_iota(jnp.int32, (cells_y, LANES), 1)
    for x in range(cells_x):
        packed = jnp.zeros((cells_y, LANES), F32)
        for v in range(VARIABLES):
            both = jnp.where(lane < LANES // 2, u_ref[v, x, :, :LANES], u_ref[v, x, :, cells_z - LANES :])
            packed = jnp.where(lane >> 3 == v, pltpu.roll(both, 8 * v + WIDTH, 1), packed)
        face_ref[x * cells_y : (x + 1) * cells_y, :] = packed
    pltpu.make_async_copy(tail_ref, tail_ref, row_sem).wait()
    pltpu.make_async_copy(head_ref, head_ref, row_sem).wait()


def pack(conserved):
    _, cells_x, cells_y, cells_z = conserved.shape
    rows = jax.ShapeDtypeStruct((WIDTH, VARIABLES, cells_x, cells_z), F32)
    return pl.pallas_call(
        pack_kernel,
        out_shape=[rows, rows, jax.ShapeDtypeStruct((cells_x * cells_y, LANES), F32)],
        in_specs=[pl.BlockSpec(memory_space=pltpu.VMEM)],
        out_specs=[pl.BlockSpec(memory_space=pltpu.VMEM)] * 3,
        scratch_shapes=[pltpu.SemaphoreType.DMA(())],
        compiler_params=pltpu.CompilerParams(vmem_limit_bytes=16 << 20),
        cost_estimate=pl.CostEstimate(flops=4_000_000, bytes_accessed=9_000_000, transcendentals=0),
        name="pack",
    )(conserved)


def exchange_z(packed):
    count = lax.axis_size("gz")
    if count == 1:
        return packed
    ahead = [(i, (i + 1) % count) for i in range(count)]
    from_left = lax.ppermute(packed, "gz", ahead)
    if count == 2:
        return from_left
    from_right = lax.ppermute(packed, "gz", [(b, a) for a, b in ahead])
    lane = jnp.arange(LANES, dtype=jnp.int32)[None, :]
    return jnp.where(lane & 7 < WIDTH, from_left, from_right)


def spread_matrix(matrix):
    rows = VARIABLES * GROUP
    pick = lax.broadcasted_iota(jnp.int32, (rows, VARIABLES), 0) >> 4
    pick = (pick == lax.broadcasted_iota(jnp.int32, (rows, VARIABLES), 1)).astype(F32)
    tall = jnp.dot(pick, matrix, precision=lax.Precision.HIGHEST, preferred_element_type=F32)
    wide = lax.dot_general(
        tall, pick, (((1,), (1,)), ((), ())), precision=lax.Precision.HIGHEST, preferred_element_type=F32
    )
    row = lax.broadcasted_iota(jnp.int32, (rows, rows), 0) & (GROUP - 1)
    column = lax.broadcasted_iota(jnp.int32, (rows, rows), 1) & (GROUP - 1)
    return split(jnp.where(row == column, wide, 0.0))


def stencil(offset):
    size = jnp.abs(offset)
    weight = jnp.where(size == 1, 45.0, jnp.where(size == 2, -9.0, jnp.where(size == 3, 1.0, 0.0)))
    return jnp.where(offset < 0, -weight, weight)


def shock_kernel(
    list_ref,
    count_ref,
    u_ref,
    face_ref,
    left_ref,
    right_ref,
    row_ref,
    change_ref,
    hot_ref,
    edge_ref,
    state_ref,
    pencils,
    turned,
    speed_t,
    press_t,
    g_out,
    g_in,
    delta,
    triple,
    smooth,
    curve,
    third,
    faces,
    edge_t,
    picked_sem,
):
    _, cells_x, cells_y, cells_z = u_ref.shape
    slots = row_ref.shape[1]
    total = cells_x * cells_y
    span = turned.shape[1]

    def fetch(p, carry):
        place = list_ref[p]
        pltpu.make_async_copy(
            u_ref.at[:, place // cells_y, pl.ds(place % cells_y, 1), :], pencils.at[:, pl.ds(p, 1), :], picked_sem
        ).start()
        return carry

    lax.fori_loop(0, slots, fetch, 0)
    left_high, left_low = spread_matrix(0.5 * left_ref[...])
    right_high, right_low = spread_matrix((time_step / 3.0) * right_ref[...])
    live = count_ref[0]
    lane_slots = lax.broadcasted_iota(jnp.int32, (1, slots), 1)
    wanted = jnp.where(lane_slots < live, row_ref[...], -1)
    scale = time_step / 60.0

    for begin in range(0, total, LANES):
        edge_t[:, begin : begin + LANES] = face_ref[begin : begin + LANES, :].T
    fluxes = flux_of([edge_t[8 * v : 8 * v + 8, :] for v in range(VARIABLES)], 2)
    for v in range(VARIABLES):
        edge_t[8 * v : 8 * v + 8, :] = fluxes[v]
    row = lax.broadcasted_iota(jnp.int32, (LANES, LANES), 0)
    column = lax.broadcasted_iota(jnp.int32, (LANES, LANES), 1)
    target, source = row & 7, column & 7
    reach = jnp.logical_xor(target < WIDTH, source < WIDTH)
    reach = reach & (target < 2 * WIDTH) & (source < 2 * WIDTH) & (row >> 3 == column >> 3)
    weights = jnp.where(reach, stencil(source - target), 0.0).astype(BF16)
    for begin in range(0, total, LANES):
        wide = slice(begin, begin + LANES)
        high, low = split(edge_t[:, wide])
        pencil = begin + lax.broadcasted_iota(jnp.int32, (LANES, slots), 0)
        hot = (wanted == pencil).astype(F32)
        calm = scale - scale * jnp.sum(hot, axis=1, keepdims=True)
        edge_ref[wide, :] = (dot(weights, high) + dot(weights, low)).T * calm
        hot = hot.astype(BF16)
        hot_ref[wide, :slots] = hot
        hot_ref[wide, slots:] = hot

    def neighbour(p, carry):
        speed_t[pl.ds(p, 1), :] = face_ref[pl.ds(list_ref[p], 1), :]
        return carry

    lax.fori_loop(0, slots, neighbour, 0, unroll=8)
    border = speed_t[0:slots, :].T

    def state(index, carry):
        at = slice(index * 8, index * 8 + 8)
        x, y = index * 8 // cells_y, index * 8 % cells_y
        pencil = index * 8 + lax.broadcasted_iota(jnp.int32, (8, slots), 0)
        calm = scale - scale * jnp.sum((wanted == pencil).astype(F32), axis=1, keepdims=True)
        for begin in range(0, cells_z, LANES):
            wide = slice(begin, begin + LANES)
            parts = [u_ref[v, x, y : y + 8, wide] for v in range(VARIABLES)]
            inverse, pressure = state_of(parts)
            state_ref[0, at, wide] = parts[SPECIES + 1] * (inverse * scale)
            state_ref[1, at, wide] = parts[SPECIES + 2] * (inverse * calm)
            state_ref[2, at, wide] = pressure
            state_ref[3, at, wide] = pressure * calm
        return carry

    for index in range(total // 8):
        state(index, 0)

    pltpu.make_async_copy(pencils, pencils, picked_sem).wait()
    for v in range(VARIABLES):
        tile = border[8 * v : 8 * v + 8, :]
        turned[v, 0:LEAD, :] = tile
        turned[v, span - 8 : span, :] = tile
        turned[v, LEAD - WIDTH : LEAD - WIDTH + 8, :] = tile
        turned[v, LEAD + cells_z - WIDTH : LEAD + cells_z - WIDTH + 8, :] = tile
        for begin in range(0, cells_z, LANES):
            turned[v, LEAD + begin : LEAD + begin + LANES, :] = pencils[v, :, begin : begin + LANES].T

    top = jnp.zeros((8, slots), F32)
    for begin in range(0, span, 8):
        parts = [turned[v, begin : begin + 8, :] for v in range(VARIABLES)]
        inverse, pressure = state_of(parts)
        velocity = parts[SPECIES + 2] * inverse
        speed_t[begin : begin + 8, :] = 0.5 * velocity
        press_t[begin : begin + 8, :] = pressure
        size = jnp.abs(velocity)
        if begin < LEAD - WIDTH or begin + 8 > LEAD + cells_z + WIDTH:
            at = begin + lax.broadcasted_iota(jnp.int32, (8, slots), 0)
            size = jnp.where((at >= LEAD - WIDTH) & (at < LEAD + cells_z + WIDTH), size, 0.0)
        top = jnp.maximum(top, size)
    wave = 0.5 * (jnp.max(top, axis=0, keepdims=True) + 1.0)

    def project(index, carry):
        at = pl.ds(pl.multiple_of(index * GROUP, GROUP), GROUP)
        velocity = speed_t[at, :]
        pressure = press_t[at, :]
        parts = [turned[v, at, :] for v in range(VARIABLES)]
        flux = [part * velocity for part in parts]
        flux[SPECIES + 2] = flux[SPECIES + 2] + 0.5 * pressure
        flux[SPECIES + 3] = flux[SPECIES + 3] + pressure * velocity
        high, low = [], []
        for v in range(VARIABLES):
            one, two = split(jnp.concatenate([flux[v], wave * parts[v]], axis=1))
            high.append(one)
            low.append(two)
        high = jnp.concatenate(high, axis=0)
        low = jnp.concatenate(low, axis=0)
        both = dot(left_high, high) + dot(left_high, low) + dot(left_low, high)
        both = both.reshape(VARIABLES, GROUP, 2 * slots)
        g_out[:, at, :] = both[:, :, :slots] + both[:, :, slots:]
        g_in[:, at, :] = both[:, :, :slots] - both[:, :, slots:]
        return carry

    lax.fori_loop(0, span // GROUP, project, 0, unroll=True)

    def upwind(i, carry):
        for side, source in enumerate((g_out, g_in)):
            for begin in range(0, span, 8):
                step = source[i, begin + 1 : begin + 9, :] - source[i, begin : begin + 8, :]
                delta[side, begin : begin + 8, :] = step
                triple[side, begin : begin + 8, :] = 3.0 * step
            for begin in range(1, span, 8):
                bend = delta[side, begin : begin + 8, :] - delta[side, begin - 1 : begin + 7, :]
                curve[side, begin : begin + 8, :] = bend
                smooth[side, begin : begin + 8, :] = (13.0 / 3.0 * bend) * bend + weno_epsilon
            for begin in range(0, span, 8):
                third[side, begin : begin + 8, :] = (
                    curve[side, begin + 1 : begin + 9, :] - curve[side, begin : begin + 8, :]
                )
        for begin in range(0, cells_z + 8, 8):
            at = begin + LEAD - 1

            def read(ref, side, offset):
                return ref[side, at + offset : at + offset + 8, :]

            value = None
            for side, source in enumerate((g_out, g_in)):
                if side == 0:
                    d1, d2, d3, d4 = (read(delta, 0, o) for o in (-2, -1, 0, 1))
                    three2, three3 = read(triple, 0, -1), read(triple, 0, 0)
                    s1, s2, s3 = (read(smooth, 0, o) for o in (-1, 0, 1))
                    u1, u2 = (read(third, 0, o) for o in (-1, 0))
                else:
                    d1, d2, d3, d4 = (read(delta, 1, o) for o in (2, 1, 0, -1))
                    three2, three3 = read(triple, 1, 1), read(triple, 1, 0)
                    s1, s2, s3 = (read(smooth, 1, o) for o in (2, 1, 0))
                    u1, u2 = (read(third, 1, o) for o in (1, 0))
                centre = source[i, at + side : at + side + 8, :]
                t0 = three2 - d1
                t1 = d2 + d3
                t2 = d4 - three3
                r0 = pl.reciprocal(s1 + t0 * t0, approx=True)
                r1 = pl.reciprocal(s2 + t1 * t1, approx=True)
                r2 = pl.reciprocal(s3 + t2 * t2, approx=True)
                w0 = r0 * (r0 * (1.0 / 3.0))
                w1 = r1 * r1
                w2 = r2 * r2
                above = (w0 + w0) * u1 + w2 * u2
                below = (w0 + w2) + (w1 + w1)
                bent = above * pl.reciprocal(below, approx=True)
                line = t1 + d3
                if side == 0:
                    value = 6.0 * centre + line - bent
                else:
                    value = value + (6.0 * centre - line + bent)
            faces[i, begin : begin + 8, :] = value
        return carry

    lax.fori_loop(0, VARIABLES, upwind, 0)

    keep = lane_slots < live

    def back(index, carry):
        base = pl.multiple_of(index * 2 * GROUP, 2 * GROUP)
        high, low = [], []
        for v in range(VARIABLES):
            pieces = []
            for begin in (0, GROUP):
                here = faces[v, pl.ds(base + begin, GROUP), :]
                after = faces[v, pl.ds(base + begin + 1, GROUP), :]
                pieces.append(after - here)
            one, two = split(jnp.concatenate(pieces, axis=1))
            high.append(one)
            low.append(two)
        high = jnp.concatenate(high, axis=0)
        low = jnp.concatenate(low, axis=0)
        both = dot(right_high, high) + dot(right_high, low) + dot(right_low, high)
        both = both.reshape(VARIABLES, GROUP, 2 * slots)
        for part, begin in enumerate((0, GROUP)):
            piece = jnp.where(keep[None], both[:, :, part * slots : part * slots + slots], 0.0)
            one, two = split(piece)
            change_ref[:, pl.ds(base + begin, GROUP), :slots] = one
            change_ref[:, pl.ds(base + begin, GROUP), slots:] = two
        return carry

    lax.fori_loop(0, cells_z // (2 * GROUP), back, 0, unroll=True)


def shock(listed, count, conserved, face, char_left, char_right):
    _, cells_x, cells_y, cells_z = conserved.shape
    slots = listed.shape[0]
    total = cells_x * cells_y
    span = -(-(cells_z + 2 * LEAD) // GROUP) * GROUP
    vmem = pltpu.VMEM
    work = vmem((2, span + 8, slots), F32)
    scratch = [
        vmem((VARIABLES, slots, cells_z), F32),
        vmem((VARIABLES, span, slots), F32),
        vmem((span, slots), F32),
        vmem((span, slots), F32),
        vmem((VARIABLES, span + 8, slots), F32),
        vmem((VARIABLES, span + 8, slots), F32),
        work,
        work,
        work,
        work,
        work,
        vmem((VARIABLES, cells_z + 8, slots), F32),
        vmem((LANES, total), F32),
        pltpu.SemaphoreType.DMA(()),
    ]
    smem = pl.BlockSpec(memory_space=pltpu.SMEM)
    whole = pl.BlockSpec(memory_space=pltpu.VMEM)
    return pl.pallas_call(
        shock_kernel,
        out_shape=[
            jax.ShapeDtypeStruct((VARIABLES, cells_z, 2 * slots), BF16),
            jax.ShapeDtypeStruct((total, 2 * slots), BF16),
            jax.ShapeDtypeStruct((total, LANES), F32),
            jax.ShapeDtypeStruct((4, total, cells_z), F32),
        ],
        in_specs=[smem, smem, whole, whole, whole, whole, whole],
        out_specs=[whole] * 4,
        scratch_shapes=scratch,
        compiler_params=pltpu.CompilerParams(vmem_limit_bytes=24 << 20),
        cost_estimate=pl.CostEstimate(flops=6_000_000_000, bytes_accessed=14_000_000, transcendentals=4_000_000),
        name="shock",
    )(listed, count, conserved, face, char_left, char_right, listed.reshape(1, slots))


def advance_kernel(
    u_ref,
    change_ref,
    hot_ref,
    edge_ref,
    state_ref,
    before_ref,
    after_ref,
    out_ref,
    done,
    fluxes,
    along_y,
    around,
    band,
    out_sem,
):
    _, total, cells_z = u_ref.shape
    cells_x = before_ref.shape[2]
    cells_y = total // cells_x
    pitch = cells_y + 16
    halves = cells_z // LANES
    scale = time_step / 60.0

    row = lax.broadcasted_iota(jnp.int32, (cells_z, cells_z), 0)
    column = lax.broadcasted_iota(jnp.int32, (cells_z, cells_z), 1)
    weights = stencil(row - column).astype(BF16)
    band[:cells_z, :] = weights
    band[cells_z:, :] = weights
    for side, source in enumerate((before_ref, after_ref)):
        for j in range(WIDTH):
            for half in range(halves):
                wide = slice(half * LANES, half * LANES + LANES)
                parts = [source[j, i, :, wide] for i in range(VARIABLES)]
                inverse, pressure = state_of(parts)
                around[side, j, 0, :, wide] = parts[SPECIES + 1] * (inverse * scale)
                around[side, j, 1, :, wide] = pressure

    lane = lax.broadcasted_iota(jnp.int32, (GROUP, LANES), 1)
    rows = min(total, 256)
    for v in range(VARIABLES):
        turn = v % 2

        def flux_y(value, speed, pressure):
            if v == SPECIES + 1:
                return value * speed + scale * pressure
            if v == SPECIES + 3:
                return (value + pressure) * speed
            return value * speed

        def flux_z(value, at, wide):
            if v == SPECIES + 2:
                return value * state_ref[1, at, wide] + state_ref[3, at, wide]
            if v == SPECIES + 3:
                return (value + state_ref[2, at, wide]) * state_ref[1, at, wide]
            return value * state_ref[1, at, wide]

        for side, source in enumerate((before_ref, after_ref)):
            for j in range(WIDTH):
                begin = 8 - WIDTH + j if side == 0 else 8 + cells_y + j
                for half in range(halves):
                    wide = slice(half * LANES, half * LANES + LANES)
                    along_y[turn, half, pl.ds(begin, cells_x, stride=pitch), :] = flux_y(
                        source[j, v, :, wide], around[side, j, 0, :, wide], around[side, j, 1, :, wide]
                    )
        for begin in range(0, total, GROUP):
            at = slice(begin, begin + GROUP)
            place = begin // cells_y * pitch + 8 + begin % cells_y
            for half in range(halves):
                wide = slice(half * LANES, half * LANES + LANES)
                value = u_ref[v, at, wide]
                along_y[turn, half, place : place + GROUP, :] = flux_y(
                    value, state_ref[0, at, wide], state_ref[2, at, wide]
                )
                high, low = split(flux_z(value, at, wide))
                fluxes[turn, at, half * LANES : half * LANES + LANES] = high
                fluxes[turn, at, cells_z + half * LANES : cells_z + half * LANES + LANES] = low
        for base in range(0, total, rows):
            gained = dot(fluxes[turn, base : base + rows, :], band[...])
            gained = gained + lax.dot_general(
                hot_ref[base : base + rows, :], change_ref[v], (((1,), (1,)), ((), ())), preferred_element_type=F32
            )
            for begin in range(base, base + rows, GROUP):
                at = slice(begin, begin + GROUP)
                place = begin // cells_y * pitch + 8 + begin % cells_y
                border = pltpu.roll(edge_ref[at, :], (LANES - WIDTH - 8 * v) % LANES, 1)
                for half in range(halves):
                    wide = slice(half * LANES, half * LANES + LANES)

                    def read(offset):
                        return along_y[turn, half, place + offset : place + offset + GROUP, :]

                    value = u_ref[v, at, wide] - gained[begin - base : begin - base + GROUP, wide]
                    value = value - (
                        45.0 * (read(1) - read(-1)) - 9.0 * (read(2) - read(-2)) + (read(3) - read(-3))
                    )
                    if half == 0:
                        value = value - jnp.where(lane < WIDTH, border, 0.0)
                    if half == halves - 1:
                        value = value - jnp.where(lane >= LANES - WIDTH, border, 0.0)
                    done[v, at, wide] = value
        pltpu.make_async_copy(done.at[v], out_ref.at[v], out_sem).start()
    pltpu.make_async_copy(done, done, out_sem).wait()


def advance(conserved, change, hot, edge, state, before, after):
    _, cells_x, cells_y, cells_z = conserved.shape
    total = cells_x * cells_y
    whole = pl.BlockSpec(memory_space=pltpu.VMEM)
    result = pl.pallas_call(
        advance_kernel,
        out_shape=jax.ShapeDtypeStruct((VARIABLES, total, cells_z), F32),
        in_specs=[whole] * 7,
        out_specs=pl.BlockSpec(memory_space=pl.ANY),
        scratch_shapes=[
            pltpu.VMEM((VARIABLES, total, cells_z), F32),
            pltpu.VMEM((2, total, 2 * cells_z), BF16),
            pltpu.VMEM((2, cells_z // LANES, cells_x * (cells_y + 16), LANES), F32),
            pltpu.VMEM((2, WIDTH, 2, cells_x, cells_z), F32),
            pltpu.VMEM((2 * cells_z, cells_z), BF16),
            pltpu.SemaphoreType.DMA(()),
        ],
        compiler_params=pltpu.CompilerParams(vmem_limit_bytes=24 << 20),
        cost_estimate=pl.CostEstimate(flops=4_000_000_000, bytes_accessed=20_000_000, transcendentals=0),
        name="advance",
    )(conserved.reshape(VARIABLES, total, cells_z), change, hot, edge, state, before, after)
    return result.reshape(conserved.shape)


def on_device(conserved, char_left, char_right, shock_list, shock_count):
    slots = shock_list.shape[-1]
    count = lax.axis_size("gy")
    ahead = [(i, (i + 1) % count) for i in range(count)]
    tail, head, packed = pack(conserved)
    before = lax.ppermute(tail, "gy", ahead)
    after = lax.ppermute(head, "gy", [(b, a) for a, b in ahead])
    face = exchange_z(packed)
    change, hot, edge, state = shock(
        shock_list.reshape(slots), shock_count.reshape(1), conserved, face, char_left, char_right
    )
    return advance(conserved, change, hot, edge, state, before, after)


def solution(mesh):
    placed = (P(None, "gx", "gy", "gz"), P(), P(), P("gx", "gy", "gz", None), P("gx", "gy", "gz"))
    return jax.shard_map(
        on_device, mesh=mesh, in_specs=placed, out_specs=P(None, "gx", "gy", "gz"), check_vma=False
    )
```

```python
import functools

import jax
import jax.numpy as jnp
from jax import lax
from jax.experimental import pallas as pl
from jax.experimental.pallas import tpu as pltpu
from jax.sharding import PartitionSpec as P

SPECIES = 9
VARIABLES = 14
WIDTH = 3
GROUP = 16
LANES = 128
LEAD = 8

gas_excess = 0.4
time_step = 0.2
weno_epsilon = 1e-06

F32 = jnp.float32
BF16 = jnp.bfloat16


def split(values):
    high = values.astype(BF16)
    low = (values - high.astype(F32)).astype(BF16)
    return high, low


def dot(left, right):
    return jnp.dot(left, right, preferred_element_type=F32)


def state_of(parts):
    density = parts[0]
    for index in range(1, SPECIES):
        density = density + parts[index]
    inverse = pl.reciprocal(density, approx=True)
    first, second, last = parts[SPECIES], parts[SPECIES + 1], parts[SPECIES + 2]
    kinetic = 0.5 * (first * first + second * second + last * last) * inverse
    pressure = gas_excess * (parts[SPECIES + 3] - parts[SPECIES + 4] - kinetic)
    return inverse, pressure


def flux_of(parts, normal):
    inverse, pressure = state_of(parts)
    velocity = parts[SPECIES + normal] * inverse
    result = [part * velocity for part in parts]
    result[SPECIES + normal] = result[SPECIES + normal] + pressure
    result[SPECIES + 3] = result[SPECIES + 3] + pressure * velocity
    return result


def pack_kernel(u_ref, tail_ref, head_ref, face_ref, row_sem):
    _, cells_x, cells_y, cells_z = u_ref.shape
    for x in range(cells_x):
        for j in range(WIDTH):
            pltpu.make_async_copy(
                u_ref.at[:, x, pl.ds(cells_y - WIDTH + j, 1), :], tail_ref.at[j, :, pl.ds(x, 1), :], row_sem
            ).start()
            pltpu.make_async_copy(
                u_ref.at[:, x, pl.ds(j, 1), :], head_ref.at[j, :, pl.ds(x, 1), :], row_sem
            ).start()
    lane = lax.broadcasted_iota(jnp.int32, (cells_y, LANES), 1)
    for x in range(cells_x):
        packed = jnp.zeros((cells_y, LANES), F32)
        for v in range(VARIABLES):
            both = jnp.where(lane < LANES // 2, u_ref[v, x, :, :LANES], u_ref[v, x, :, cells_z - LANES :])
            packed = jnp.where(lane >> 3 == v, pltpu.roll(both, 8 * v + WIDTH, 1), packed)
        face_ref[x * cells_y : (x + 1) * cells_y, :] = packed
    pltpu.make_async_copy(tail_ref, tail_ref, row_sem).wait()
    pltpu.make_async_copy(head_ref, head_ref, row_sem).wait()


def pack(conserved):
    _, cells_x, cells_y, cells_z = conserved.shape
    rows = jax.ShapeDtypeStruct((WIDTH, VARIABLES, cells_x, cells_z), F32)
    return pl.pallas_call(
        pack_kernel,
        out_shape=[
            rows,
            rows,
            jax.ShapeDtypeStruct((cells_x * cells_y, LANES), F32),
        ],
        in_specs=[pl.BlockSpec(memory_space=pltpu.VMEM)],
        out_specs=[pl.BlockSpec(memory_space=pltpu.VMEM)] * 3,
        scratch_shapes=[pltpu.SemaphoreType.DMA(())],
        compiler_params=pltpu.CompilerParams(vmem_limit_bytes=16 << 20),
        cost_estimate=pl.CostEstimate(flops=4_000_000, bytes_accessed=9_000_000, transcendentals=0),
        name="pack",
    )(conserved)


def exchange_z(packed):
    count = lax.axis_size("gz")
    if count == 1:
        return packed
    ahead = [(i, (i + 1) % count) for i in range(count)]
    from_left = lax.ppermute(packed, "gz", ahead)
    if count == 2:
        return from_left
    from_right = lax.ppermute(packed, "gz", [(b, a) for a, b in ahead])
    lane = jnp.arange(LANES, dtype=jnp.int32)[None, :]
    return jnp.where(lane & 7 < WIDTH, from_left, from_right)


def spread_matrix(matrix):
    rows = VARIABLES * GROUP
    pick = lax.broadcasted_iota(jnp.int32, (rows, VARIABLES), 0) >> 4
    pick = (pick == lax.broadcasted_iota(jnp.int32, (rows, VARIABLES), 1)).astype(F32)
    tall = jnp.dot(pick, matrix, precision=lax.Precision.HIGHEST, preferred_element_type=F32)
    wide = lax.dot_general(
        tall, pick, (((1,), (1,)), ((), ())), precision=lax.Precision.HIGHEST, preferred_element_type=F32
    )
    row = lax.broadcasted_iota(jnp.int32, (rows, rows), 0) & (GROUP - 1)
    column = lax.broadcasted_iota(jnp.int32, (rows, rows), 1) & (GROUP - 1)
    return split(jnp.where(row == column, wide, 0.0))


def stencil(offset):
    size = jnp.abs(offset)
    weight = jnp.where(size == 1, 45.0, jnp.where(size == 2, -9.0, jnp.where(size == 3, 1.0, 0.0)))
    return jnp.where(offset < 0, -weight, weight)


def shock_kernel(
    list_ref,
    count_ref,
    u_ref,
    face_ref,
    left_ref,
    right_ref,
    row_ref,
    change_ref,
    hot_ref,
    edge_ref,
    state_ref,
    pencils,
    turned,
    speed_t,
    press_t,
    g_out,
    g_in,
    delta,
    triple,
    smooth,
    curve,
    third,
    faces,
    edge_t,
):
    _, cells_x, cells_y, cells_z = u_ref.shape
    slots = row_ref.shape[-1]
    total = cells_x * cells_y
    span = turned.shape[1]

    def fetch(p):
        place = list_ref[0, 0, 0, p]
        x, y = place // cells_y, place % cells_y
        for v in range(VARIABLES):
            pencils[v, pl.ds(p, 1), :] = u_ref[v, x, pl.ds(y, 1), :]


    live = count_ref[0, 0, 0]
    lane_slots = lax.broadcasted_iota(jnp.int32, (1, slots), 1)
    wanted = jnp.where(lane_slots < live, row_ref[0, 0], -1)
    scale = time_step / 60.0

    for begin in range(0, total, LANES):
        edge_t[:, begin : begin + LANES] = face_ref[begin : begin + LANES, :].T
    fluxes = flux_of([edge_t[8 * v : 8 * v + 8, :] for v in range(VARIABLES)], 2)
    for v in range(VARIABLES):
        edge_t[8 * v : 8 * v + 8, :] = fluxes[v]
    row = lax.broadcasted_iota(jnp.int32, (LANES, LANES), 0)
    column = lax.broadcasted_iota(jnp.int32, (LANES, LANES), 1)
    target, source = row & 7, column & 7
    reach = jnp.logical_xor(target < WIDTH, source < WIDTH)
    reach = reach & (target < 2 * WIDTH) & (source < 2 * WIDTH) & (row >> 3 == column >> 3)
    weights = jnp.where(reach, stencil(source - target), 0.0).astype(BF16)
    for begin in range(0, total, LANES):
        wide = slice(begin, begin + LANES)
        high, low = split(edge_t[:, wide])
        pencil = begin + lax.broadcasted_iota(jnp.int32, (LANES, slots), 0)
        hot = (wanted == pencil).astype(F32)
        calm = scale - scale * jnp.sum(hot, axis=1, keepdims=True)
        edge_ref[wide, :] = (dot(weights, high) + dot(weights, low)).T * calm
        hot = hot.astype(BF16)
        hot_ref[wide, :slots] = hot
        hot_ref[wide, slots:] = hot

    left_high, left_low = spread_matrix(0.5 * left_ref[...])
    right_high, right_low = spread_matrix((time_step / 3.0) * right_ref[...])

    def neighbour(p, carry):
        speed_t[pl.ds(p, 1), :] = face_ref[pl.ds(list_ref[0, 0, 0, p], 1), :]
        return carry

    lax.fori_loop(0, slots, neighbour, 0, unroll=8)
    border = speed_t[0:slots, :].T

    def state(index, carry):
        at = slice(index * 8, index * 8 + 8)
        x, y = index * 8 // cells_y, index * 8 % cells_y
        pencil = index * 8 + lax.broadcasted_iota(jnp.int32, (8, slots), 0)
        calm = scale - scale * jnp.sum((wanted == pencil).astype(F32), axis=1, keepdims=True)
        for begin in range(0, cells_z, LANES):
            wide = slice(begin, begin + LANES)
            parts = [u_ref[v, x, y : y + 8, wide] for v in range(VARIABLES)]
            inverse, pressure = state_of(parts)
            state_ref[0, at, wide] = parts[SPECIES + 1] * (inverse * scale)
            state_ref[1, at, wide] = parts[SPECIES + 2] * (inverse * calm)
            state_ref[2, at, wide] = pressure
            state_ref[3, at, wide] = pressure * calm
        return carry

    for index in range(total // 8):
        state(index, 0)
        for p in range(index * 8 * slots // total, (index + 1) * 8 * slots // total):
            fetch(p)

    for v in range(VARIABLES):
        tile = border[8 * v : 8 * v + 8, :]
        turned[v, 0:LEAD, :] = tile
        turned[v, span - 8 : span, :] = tile
        turned[v, LEAD - WIDTH : LEAD - WIDTH + 8, :] = tile
        turned[v, LEAD + cells_z - WIDTH : LEAD + cells_z - WIDTH + 8, :] = tile
        for begin in range(0, cells_z, LANES):
            turned[v, LEAD + begin : LEAD + begin + LANES, :] = pencils[v, :, begin : begin + LANES].T

    top = jnp.zeros((8, slots), F32)
    for begin in range(0, span, 8):
        parts = [turned[v, begin : begin + 8, :] for v in range(VARIABLES)]
        inverse, pressure = state_of(parts)
        velocity = parts[SPECIES + 2] * inverse
        speed_t[begin : begin + 8, :] = 0.5 * velocity
        press_t[begin : begin + 8, :] = pressure
        size = jnp.abs(velocity)
        if begin < LEAD - WIDTH or begin + 8 > LEAD + cells_z + WIDTH:
            at = begin + lax.broadcasted_iota(jnp.int32, (8, slots), 0)
            size = jnp.where((at >= LEAD - WIDTH) & (at < LEAD + cells_z + WIDTH), size, 0.0)
        top = jnp.maximum(top, size)
    wave = 0.5 * (jnp.max(top, axis=0, keepdims=True) + 1.0)

    def project(index, carry):
        at = pl.ds(pl.multiple_of(index * GROUP, GROUP), GROUP)
        velocity = speed_t[at, :]
        pressure = press_t[at, :]
        parts = [turned[v, at, :] for v in range(VARIABLES)]
        flux = [part * velocity for part in parts]
        flux[SPECIES + 2] = flux[SPECIES + 2] + 0.5 * pressure
        flux[SPECIES + 3] = flux[SPECIES + 3] + pressure * velocity
        high, low = [], []
        for v in range(VARIABLES):
            one, two = split(jnp.concatenate([flux[v], wave * parts[v]], axis=1))
            high.append(one)
            low.append(two)
        high = jnp.concatenate(high, axis=0)
        low = jnp.concatenate(low, axis=0)
        both = dot(left_high, high) + dot(left_high, low) + dot(left_low, high)
        both = both.reshape(VARIABLES, GROUP, 2 * slots)
        g_out[:, at, :] = both[:, :, :slots] + both[:, :, slots:]
        g_in[:, at, :] = both[:, :, :slots] - both[:, :, slots:]
        return carry

    lax.fori_loop(0, span // GROUP, project, 0, unroll=True)

    def upwind(i, carry):
        for side, source in enumerate((g_out, g_in)):
            for begin in range(0, span, 8):
                step = source[i, begin + 1 : begin + 9, :] - source[i, begin : begin + 8, :]
                delta[side, begin : begin + 8, :] = step
                triple[side, begin : begin + 8, :] = 3.0 * step
            for begin in range(1, span, 8):
                bend = delta[side, begin : begin + 8, :] - delta[side, begin - 1 : begin + 7, :]
                curve[side, begin : begin + 8, :] = bend
                smooth[side, begin : begin + 8, :] = (13.0 / 3.0 * bend) * bend + weno_epsilon
            for begin in range(0, span, 8):
                third[side, begin : begin + 8, :] = (
                    curve[side, begin + 1 : begin + 9, :] - curve[side, begin : begin + 8, :]
                )
        for begin in range(0, cells_z + 8, 8):
            at = begin + LEAD - 1

            def read(ref, side, offset):
                return ref[side, at + offset : at + offset + 8, :]

            value = None
            for side, source in enumerate((g_out, g_in)):
                if side == 0:
                    d1, d2, d3, d4 = (read(delta, 0, o) for o in (-2, -1, 0, 1))
                    three2, three3 = read(triple, 0, -1), read(triple, 0, 0)
                    s1, s2, s3 = (read(smooth, 0, o) for o in (-1, 0, 1))
                    u1, u2 = (read(third, 0, o) for o in (-1, 0))
                else:
                    d1, d2, d3, d4 = (read(delta, 1, o) for o in (2, 1, 0, -1))
                    three2, three3 = read(triple, 1, 1), read(triple, 1, 0)
                    s1, s2, s3 = (read(smooth, 1, o) for o in (2, 1, 0))
                    u1, u2 = (read(third, 1, o) for o in (1, 0))
                centre = source[i, at + side : at + side + 8, :]
                t0 = three2 - d1
                t1 = d2 + d3
                t2 = d4 - three3
                r0 = pl.reciprocal(s1 + t0 * t0, approx=True)
                r1 = pl.reciprocal(s2 + t1 * t1, approx=True)
                r2 = pl.reciprocal(s3 + t2 * t2, approx=True)
                w0 = r0 * (r0 * (1.0 / 3.0))
                w1 = r1 * r1
                w2 = r2 * r2
                above = (w0 + w0) * u1 + w2 * u2
                below = (w0 + w2) + (w1 + w1)
                bent = above * pl.reciprocal(below, approx=True)
                line = t1 + d3
                if side == 0:
                    value = 6.0 * centre + line - bent
                else:
                    value = value + (6.0 * centre - line + bent)
            faces[i, begin : begin + 8, :] = value
        return carry

    lax.fori_loop(0, VARIABLES, upwind, 0)

    keep = lane_slots < live

    def back(index, carry):
        base = pl.multiple_of(index * 2 * GROUP, 2 * GROUP)
        high, low = [], []
        for v in range(VARIABLES):
            pieces = []
            for begin in (0, GROUP):
                here = faces[v, pl.ds(base + begin, GROUP), :]
                after = faces[v, pl.ds(base + begin + 1, GROUP), :]
                pieces.append(after - here)
            one, two = split(jnp.concatenate(pieces, axis=1))
            high.append(one)
            low.append(two)
        high = jnp.concatenate(high, axis=0)
        low = jnp.concatenate(low, axis=0)
        both = dot(right_high, high) + dot(right_high, low) + dot(right_low, high)
        both = both.reshape(VARIABLES, GROUP, 2 * slots)
        for part, begin in enumerate((0, GROUP)):
            piece = jnp.where(keep[None], both[:, :, part * slots : part * slots + slots], 0.0)
            one, two = split(piece)
            change_ref[:, pl.ds(base + begin, GROUP), :slots] = one
            change_ref[:, pl.ds(base + begin, GROUP), slots:] = two
        return carry

    lax.fori_loop(0, cells_z // (2 * GROUP), back, 0, unroll=True)


def shock(listed, count, conserved, face, char_left, char_right):
    _, cells_x, cells_y, cells_z = conserved.shape
    slots = listed.shape[-1]
    total = cells_x * cells_y
    span = -(-(cells_z + 2 * LEAD) // GROUP) * GROUP
    vmem = pltpu.VMEM
    work = vmem((2, span + 8, slots), F32)
    scratch = [
        vmem((VARIABLES, slots, cells_z), F32),
        vmem((VARIABLES, span, slots), F32),
        vmem((span, slots), F32),
        vmem((span, slots), F32),
        vmem((VARIABLES, span + 8, slots), F32),
        vmem((VARIABLES, span + 8, slots), F32),
        work,
        work,
        work,
        work,
        work,
        vmem((VARIABLES, cells_z + 8, slots), F32),
        vmem((LANES, total), F32),
    ]
    smem = pl.BlockSpec(memory_space=pltpu.SMEM)
    whole = pl.BlockSpec(memory_space=pltpu.VMEM)
    return pl.pallas_call(
        shock_kernel,
        out_shape=[
            jax.ShapeDtypeStruct((VARIABLES, cells_z, 2 * slots), BF16),
            jax.ShapeDtypeStruct((total, 2 * slots), BF16),
            jax.ShapeDtypeStruct((total, LANES), F32),
            jax.ShapeDtypeStruct((4, total, cells_z), F32),
        ],
        in_specs=[smem, smem, whole, whole, whole, whole, whole],
        out_specs=[whole] * 4,
        scratch_shapes=scratch,
        compiler_params=pltpu.CompilerParams(vmem_limit_bytes=24 << 20),
        cost_estimate=pl.CostEstimate(flops=6_000_000_000, bytes_accessed=14_000_000, transcendentals=4_000_000),
        name="shock",
    )(listed, count, conserved, face, char_left, char_right, listed)


def advance_kernel(
    u_ref, change_ref, hot_ref, edge_ref, state_ref, before_ref, after_ref, out_ref, done, left, right, rim, out_sem
):
    _, total, cells_z = u_ref.shape
    cells_x = before_ref.shape[2]
    cells_y = total // cells_x
    halves = cells_z // LANES
    scale = time_step / 60.0
    rows = right.shape[2] // 2 - cells_z

    row = lax.broadcasted_iota(jnp.int32, (cells_z, cells_z), 0)
    column = lax.broadcasted_iota(jnp.int32, (cells_z, cells_z), 1)
    along_z = stencil(row - column).astype(BF16)
    row = lax.broadcasted_iota(jnp.int32, (rows, rows), 0)
    column = lax.broadcasted_iota(jnp.int32, (rows, rows), 1)
    inside = row // cells_y == column // cells_y
    along_y = jnp.where(inside, stencil(column - row), 0.0).astype(BF16)
    for turn in range(2):
        for block in range(total // rows):
            for k in range(2):
                left[turn, block, :, 2 * cells_z + k * rows : 2 * cells_z + k * rows + rows] = along_y
                right[turn, block, k * cells_z : k * cells_z + cells_z, :] = along_z

    rim[...] = jnp.zeros_like(rim)
    for half in range(halves):
        wide = slice(half * LANES, half * LANES + LANES)
        f0, f1, f2 = (flux_of([before_ref[j, v, :, wide] for v in range(VARIABLES)], 1) for j in range(WIDTH))
        for v in range(VARIABLES):
            for j, part in enumerate((45.0 * f2[v] - 9.0 * f1[v] + f0[v], f1[v] - 9.0 * f2[v], f2[v])):
                rim[v, half, pl.ds(j, cells_x, stride=2 * GROUP), :] = scale * part
        f0, f1, f2 = (flux_of([after_ref[j, v, :, wide] for v in range(VARIABLES)], 1) for j in range(WIDTH))
        for v in range(VARIABLES):
            for j, part in enumerate((f0[v], f1[v] - 9.0 * f0[v], 45.0 * f0[v] - 9.0 * f1[v] + f2[v])):
                rim[v, half, pl.ds(2 * GROUP - WIDTH + j, cells_x, stride=2 * GROUP), :] = -scale * part

    lane = lax.broadcasted_iota(jnp.int32, (GROUP, LANES), 1)
    for v in range(VARIABLES):
        turn = v % 2

        for begin in range(0, total, GROUP):
            at = slice(begin, begin + GROUP)
            block, place = begin // rows, begin % rows
            value = u_ref[v, at, :]
            flux_y = value * state_ref[0, at, :]
            flux_z = value * state_ref[1, at, :]
            if v == SPECIES + 1:
                flux_y = flux_y + scale * state_ref[2, at, :]
            if v == SPECIES + 2:
                flux_z = flux_z + state_ref[3, at, :]
            if v == SPECIES + 3:
                flux_y = flux_y + state_ref[2, at, :] * state_ref[0, at, :]
                flux_z = flux_z + state_ref[2, at, :] * state_ref[1, at, :]
            high, low = split(flux_z)
            left[turn, block, place : place + GROUP, :cells_z] = high
            left[turn, block, place : place + GROUP, cells_z : 2 * cells_z] = low
            high, low = split(flux_y)
            place = place + 2 * cells_z
            right[turn, block, place : place + GROUP, :] = high
            right[turn, block, place + rows : place + rows + GROUP, :] = low
        for block in range(total // rows):
            base = block * rows
            gained = dot(left[turn, block], right[turn, block])
            gained = gained + lax.dot_general(
                hot_ref[base : base + rows, :], change_ref[v], (((1,), (1,)), ((), ())), preferred_element_type=F32
            )
            for begin in range(base, base + rows, GROUP):
                at = slice(begin, begin + GROUP)
                x, y = begin // cells_y, begin % cells_y
                border = pltpu.roll(edge_ref[at, :], (LANES - WIDTH - 8 * v) % LANES, 1)
                for half in range(halves):
                    wide = slice(half * LANES, half * LANES + LANES)
                    value = u_ref[v, at, wide] - gained[begin - base : begin - base + GROUP, wide]
                    if half == 0:
                        value = value - jnp.where(lane < WIDTH, border, 0.0)
                    if half == halves - 1:
                        value = value - jnp.where(lane >= LANES - WIDTH, border, 0.0)
                    if y == 0:
                        value = value + rim[v, half, 2 * GROUP * x : 2 * GROUP * x + GROUP, :]
                    if y == cells_y - GROUP:
                        value = value + rim[v, half, 2 * GROUP * x + GROUP : 2 * GROUP * x + 2 * GROUP, :]
                    done[v, at, wide] = value
        pltpu.make_async_copy(done.at[v], out_ref.at[v], out_sem).start()
    pltpu.make_async_copy(done, done, out_sem).wait()


def advance(conserved, change, hot, edge, state, before, after):
    _, cells_x, cells_y, cells_z = conserved.shape
    total = cells_x * cells_y
    rows = cells_y * max(1, min(cells_x, 256 // cells_y))
    whole = pl.BlockSpec(memory_space=pltpu.VMEM)
    result = pl.pallas_call(
        advance_kernel,
        out_shape=jax.ShapeDtypeStruct((VARIABLES, total, cells_z), F32),
        in_specs=[whole] * 7,
        out_specs=pl.BlockSpec(memory_space=pl.ANY),
        scratch_shapes=[
            pltpu.VMEM((VARIABLES, total, cells_z), F32),
            pltpu.VMEM((2, total // rows, rows, 2 * (cells_z + rows)), BF16),
            pltpu.VMEM((2, total // rows, 2 * (cells_z + rows), cells_z), BF16),
            pltpu.VMEM((VARIABLES, cells_z // LANES, cells_x * 2 * GROUP, LANES), F32),
            pltpu.SemaphoreType.DMA(()),
        ],
        compiler_params=pltpu.CompilerParams(vmem_limit_bytes=24 << 20),
        cost_estimate=pl.CostEstimate(flops=4_000_000_000, bytes_accessed=20_000_000, transcendentals=0),
        name="advance",
    )(conserved.reshape(VARIABLES, total, cells_z), change, hot, edge, state, before, after)
    return result.reshape(conserved.shape)


def on_device(conserved, char_left, char_right, shock_list, shock_count):
    count = lax.axis_size("gy")
    ahead = [(i, (i + 1) % count) for i in range(count)]
    tail, head, packed = pack(conserved)
    before = lax.ppermute(tail, "gy", ahead)
    after = lax.ppermute(head, "gy", [(b, a) for a, b in ahead])
    face = exchange_z(packed)
    change, hot, edge, state = shock(
        shock_list, shock_count, conserved, face, char_left, char_right
    )
    return advance(conserved, change, hot, edge, state, before, after)


def solution(mesh):
    placed = (P(None, "gx", "gy", "gz"), P(), P(), P("gx", "gy", "gz", None), P("gx", "gy", "gz"))
    return jax.shard_map(
        on_device, mesh=mesh, in_specs=placed, out_specs=P(None, "gx", "gy", "gz"), check_vma=False
    )
```

```python
import functools

import jax
import jax.numpy as jnp
from jax import lax
from jax.experimental import pallas as pl
from jax.experimental.pallas import tpu as pltpu
from jax.sharding import PartitionSpec as P

SPECIES = 9
VARIABLES = 14
WIDTH = 3
GROUP = 16
LANES = 128
LEAD = 8

gas_excess = 0.4
time_step = 0.2
weno_epsilon = 1e-06

F32 = jnp.float32
BF16 = jnp.bfloat16


def split(values):
    high = values.astype(BF16)
    low = (values - high.astype(F32)).astype(BF16)
    return high, low


def dot(left, right):
    return jnp.dot(left, right, preferred_element_type=F32)


def state_of(parts):
    density = parts[0]
    for index in range(1, SPECIES):
        density = density + parts[index]
    inverse = pl.reciprocal(density, approx=True)
    first, second, last = parts[SPECIES], parts[SPECIES + 1], parts[SPECIES + 2]
    kinetic = 0.5 * (first * first + second * second + last * last) * inverse
    pressure = gas_excess * (parts[SPECIES + 3] - parts[SPECIES + 4] - kinetic)
    return inverse, pressure


def flux_of(parts, normal):
    inverse, pressure = state_of(parts)
    velocity = parts[SPECIES + normal] * inverse
    result = [part * velocity for part in parts]
    result[SPECIES + normal] = result[SPECIES + normal] + pressure
    result[SPECIES + 3] = result[SPECIES + 3] + pressure * velocity
    return result


def pack_y_kernel(u_ref, tail_ref, head_ref, first_ref, sem):
    cells_x, cells_y = u_ref.shape[1], u_ref.shape[2]
    for x in range(cells_x):
        for j in range(WIDTH):
            pltpu.make_async_copy(
                u_ref.at[:, x, pl.ds(cells_y - WIDTH + j, 1), :], tail_ref.at[j, :, pl.ds(x, 1), :], sem
            ).start()
            pltpu.make_async_copy(
                u_ref.at[:, x, pl.ds(j, 1), :], head_ref.at[j, :, pl.ds(x, 1), :], sem
            ).start()
    first_ref[...] = jnp.zeros_like(first_ref)
    pltpu.make_async_copy(tail_ref, tail_ref, sem).wait()
    pltpu.make_async_copy(head_ref, head_ref, sem).wait()


def pack_y(conserved):
    cells_x, cells_z = conserved.shape[1], conserved.shape[3]
    face = jax.ShapeDtypeStruct((WIDTH, VARIABLES, cells_x, cells_z), F32)
    return pl.pallas_call(
        pack_y_kernel,
        out_shape=[face, face, jax.ShapeDtypeStruct((8, LANES), F32)],
        in_specs=[pl.BlockSpec(memory_space=pl.ANY)],
        out_specs=[pl.BlockSpec(memory_space=pltpu.VMEM)] * 3,
        scratch_shapes=[pltpu.SemaphoreType.DMA(())],
        compiler_params=pltpu.CompilerParams(vmem_limit_bytes=16 << 20),
        cost_estimate=pl.CostEstimate(flops=0, bytes_accessed=2_000_000, transcendentals=0),
        name="pack_y",
    )(conserved)


def pack_z_kernel(u_ref, first_ref, basis_ref, wanted_ref, face_ref):
    _, cells_x, cells_y, cells_z = u_ref.shape
    lane = lax.broadcasted_iota(jnp.int32, (cells_y, LANES), 1)
    for x in range(cells_x):
        packed = jnp.zeros((cells_y, LANES), F32)
        for v in range(VARIABLES):
            both = jnp.where(lane < LANES // 2, u_ref[v, x, :, :LANES], u_ref[v, x, :, cells_z - LANES :])
            packed = jnp.where(lane >> 3 == v, pltpu.roll(both, 8 * v + WIDTH, 1), packed)
        face_ref[x * cells_y : (x + 1) * cells_y, :] = packed


def pack_z(conserved, first, basis, wanted):
    _, cells_x, cells_y, _ = conserved.shape
    whole = pl.BlockSpec(memory_space=pltpu.VMEM)
    return pl.pallas_call(
        pack_z_kernel,
        out_shape=jax.ShapeDtypeStruct((cells_x * cells_y, LANES), F32),
        in_specs=[whole] * 4,
        out_specs=whole,
        compiler_params=pltpu.CompilerParams(vmem_limit_bytes=16 << 20),
        cost_estimate=pl.CostEstimate(flops=4_000_000, bytes_accessed=9_000_000, transcendentals=0),
        name="pack_z",
    )(conserved, first, basis, wanted)


def exchange_z(packed):
    count = lax.axis_size("gz")
    if count == 1:
        return packed
    ahead = [(i, (i + 1) % count) for i in range(count)]
    from_left = lax.ppermute(packed, "gz", ahead)
    if count == 2:
        return from_left
    from_right = lax.ppermute(packed, "gz", [(b, a) for a, b in ahead])
    lane = jnp.arange(LANES, dtype=jnp.int32)[None, :]
    return jnp.where(lane & 7 < WIDTH, from_left, from_right)


def spread_matrix(matrix):
    rows = VARIABLES * GROUP
    pick = lax.broadcasted_iota(jnp.int32, (rows, VARIABLES), 0) >> 4
    pick = (pick == lax.broadcasted_iota(jnp.int32, (rows, VARIABLES), 1)).astype(F32)
    tall = jnp.dot(pick, matrix, precision=lax.Precision.HIGHEST, preferred_element_type=F32)
    wide = lax.dot_general(
        tall, pick, (((1,), (1,)), ((), ())), precision=lax.Precision.HIGHEST, preferred_element_type=F32
    )
    row = lax.broadcasted_iota(jnp.int32, (rows, rows), 0) & (GROUP - 1)
    column = lax.broadcasted_iota(jnp.int32, (rows, rows), 1) & (GROUP - 1)
    return split(jnp.where(row == column, wide, 0.0))


def stencil(offset):
    size = jnp.abs(offset)
    weight = jnp.where(size == 1, 45.0, jnp.where(size == 2, -9.0, jnp.where(size == 3, 1.0, 0.0)))
    return jnp.where(offset < 0, -weight, weight)


def shock_kernel(
    list_ref,
    wanted_ref,
    u_ref,
    face_ref,
    basis_ref,
    change_ref,
    hot_ref,
    edge_ref,
    state_ref,
    pencils,
    turned,
    speed_t,
    press_t,
    g_out,
    g_in,
    delta,
    triple,
    smooth,
    curve,
    third,
    faces,
    edge_t,
):
    _, cells_x, cells_y, cells_z = u_ref.shape
    slots = wanted_ref.shape[-1]
    total = cells_x * cells_y
    span = turned.shape[1]

    def fetch(p):
        place = jnp.maximum(list_ref[0, p], 0)
        x, y = place // cells_y, place % cells_y
        for v in range(VARIABLES):
            pencils[v, pl.ds(p, 1), :] = u_ref[v, x, pl.ds(y, 1), :]


    wanted = wanted_ref[...]
    scale = time_step / 60.0

    for begin in range(0, total, LANES):
        edge_t[:, begin : begin + LANES] = face_ref[begin : begin + LANES, :].T
    fluxes = flux_of([edge_t[8 * v : 8 * v + 8, :] for v in range(VARIABLES)], 2)
    for v in range(VARIABLES):
        edge_t[8 * v : 8 * v + 8, :] = fluxes[v]
    row = lax.broadcasted_iota(jnp.int32, (LANES, LANES), 0)
    column = lax.broadcasted_iota(jnp.int32, (LANES, LANES), 1)
    target, source = row & 7, column & 7
    reach = jnp.logical_xor(target < WIDTH, source < WIDTH)
    reach = reach & (target < 2 * WIDTH) & (source < 2 * WIDTH) & (row >> 3 == column >> 3)
    weights = jnp.where(reach, stencil(source - target), 0.0).astype(BF16)
    for begin in range(0, total, LANES):
        wide = slice(begin, begin + LANES)
        high, low = split(edge_t[:, wide])
        pencil = begin + lax.broadcasted_iota(jnp.int32, (LANES, slots), 0)
        hot = (wanted == pencil).astype(F32)
        calm = scale - scale * jnp.sum(hot, axis=1, keepdims=True)
        edge_ref[wide, :] = (dot(weights, high) + dot(weights, low)).T * calm
        hot = hot.astype(BF16)
        hot_ref[wide, :slots] = hot
        hot_ref[wide, slots:] = hot

    left_high, left_low = spread_matrix(basis_ref[0])
    right_high, right_low = spread_matrix(basis_ref[1])

    def neighbour(p, carry):
        speed_t[pl.ds(p, 1), :] = face_ref[pl.ds(jnp.maximum(list_ref[0, p], 0), 1), :]
        return carry

    lax.fori_loop(0, slots, neighbour, 0, unroll=8)
    border = speed_t[0:slots, :].T

    def state(index, carry):
        at = slice(index * 8, index * 8 + 8)
        x, y = index * 8 // cells_y, index * 8 % cells_y
        pencil = index * 8 + lax.broadcasted_iota(jnp.int32, (8, slots), 0)
        calm = scale - scale * jnp.sum((wanted == pencil).astype(F32), axis=1, keepdims=True)
        for begin in range(0, cells_z, LANES):
            wide = slice(begin, begin + LANES)
            parts = [u_ref[v, x, y : y + 8, wide] for v in range(VARIABLES)]
            inverse, pressure = state_of(parts)
            state_ref[0, at, wide] = parts[SPECIES + 1] * (inverse * scale)
            state_ref[1, at, wide] = parts[SPECIES + 2] * (inverse * calm)
            state_ref[2, at, wide] = pressure
            state_ref[3, at, wide] = pressure * calm
        return carry

    for index in range(total // 8):
        state(index, 0)
        for p in range(index * 8 * slots // total, (index + 1) * 8 * slots // total):
            fetch(p)

    for v in range(VARIABLES):
        tile = border[8 * v : 8 * v + 8, :]
        turned[v, 0:LEAD, :] = tile
        turned[v, span - 8 : span, :] = tile
        turned[v, LEAD - WIDTH : LEAD - WIDTH + 8, :] = tile
        turned[v, LEAD + cells_z - WIDTH : LEAD + cells_z - WIDTH + 8, :] = tile
        for begin in range(0, cells_z, LANES):
            turned[v, LEAD + begin : LEAD + begin + LANES, :] = pencils[v, :, begin : begin + LANES].T

    top = jnp.zeros((8, slots), F32)
    for begin in range(0, span, 8):
        parts = [turned[v, begin : begin + 8, :] for v in range(VARIABLES)]
        inverse, pressure = state_of(parts)
        velocity = parts[SPECIES + 2] * inverse
        speed_t[begin : begin + 8, :] = 0.5 * velocity
        press_t[begin : begin + 8, :] = pressure
        size = jnp.abs(velocity)
        if begin < LEAD - WIDTH or begin + 8 > LEAD + cells_z + WIDTH:
            at = begin + lax.broadcasted_iota(jnp.int32, (8, slots), 0)
            size = jnp.where((at >= LEAD - WIDTH) & (at < LEAD + cells_z + WIDTH), size, 0.0)
        top = jnp.maximum(top, size)
    wave = 0.5 * (jnp.max(top, axis=0, keepdims=True) + 1.0)

    def project(index, carry):
        at = pl.ds(pl.multiple_of(index * GROUP, GROUP), GROUP)
        velocity = speed_t[at, :]
        pressure = press_t[at, :]
        parts = [turned[v, at, :] for v in range(VARIABLES)]
        flux = [part * velocity for part in parts]
        flux[SPECIES + 2] = flux[SPECIES + 2] + 0.5 * pressure
        flux[SPECIES + 3] = flux[SPECIES + 3] + pressure * velocity
        high, low = [], []
        for v in range(VARIABLES):
            one, two = split(jnp.concatenate([flux[v], wave * parts[v]], axis=1))
            high.append(one)
            low.append(two)
        high = jnp.concatenate(high, axis=0)
        low = jnp.concatenate(low, axis=0)
        both = dot(left_high, high) + dot(left_high, low) + dot(left_low, high)
        both = both.reshape(VARIABLES, GROUP, 2 * slots)
        g_out[:, at, :] = both[:, :, :slots] + both[:, :, slots:]
        g_in[:, at, :] = both[:, :, :slots] - both[:, :, slots:]
        return carry

    lax.fori_loop(0, span // GROUP, project, 0, unroll=True)

    def upwind(i, carry):
        for side, source in enumerate((g_out, g_in)):
            for begin in range(0, span, 8):
                step = source[i, begin + 1 : begin + 9, :] - source[i, begin : begin + 8, :]
                delta[side, begin : begin + 8, :] = step
                triple[side, begin : begin + 8, :] = 3.0 * step
            for begin in range(1, span, 8):
                bend = delta[side, begin : begin + 8, :] - delta[side, begin - 1 : begin + 7, :]
                curve[side, begin : begin + 8, :] = bend
                smooth[side, begin : begin + 8, :] = (13.0 / 3.0 * bend) * bend + weno_epsilon
            for begin in range(0, span, 8):
                third[side, begin : begin + 8, :] = (
                    curve[side, begin + 1 : begin + 9, :] - curve[side, begin : begin + 8, :]
                )
        for begin in range(0, cells_z + 8, 8):
            at = begin + LEAD - 1

            def read(ref, side, offset):
                return ref[side, at + offset : at + offset + 8, :]

            value = None
            for side, source in enumerate((g_out, g_in)):
                if side == 0:
                    d1, d2, d3, d4 = (read(delta, 0, o) for o in (-2, -1, 0, 1))
                    three2, three3 = read(triple, 0, -1), read(triple, 0, 0)
                    s1, s2, s3 = (read(smooth, 0, o) for o in (-1, 0, 1))
                    u1, u2 = (read(third, 0, o) for o in (-1, 0))
                else:
                    d1, d2, d3, d4 = (read(delta, 1, o) for o in (2, 1, 0, -1))
                    three2, three3 = read(triple, 1, 1), read(triple, 1, 0)
                    s1, s2, s3 = (read(smooth, 1, o) for o in (2, 1, 0))
                    u1, u2 = (read(third, 1, o) for o in (1, 0))
                centre = source[i, at + side : at + side + 8, :]
                t0 = three2 - d1
                t1 = d2 + d3
                t2 = d4 - three3
                r0 = pl.reciprocal(s1 + t0 * t0, approx=True)
                r1 = pl.reciprocal(s2 + t1 * t1, approx=True)
                r2 = pl.reciprocal(s3 + t2 * t2, approx=True)
                w0 = r0 * (r0 * (1.0 / 3.0))
                w1 = r1 * r1
                w2 = r2 * r2
                above = (w0 + w0) * u1 + w2 * u2
                below = (w0 + w2) + (w1 + w1)
                bent = above * pl.reciprocal(below, approx=True)
                line = t1 + d3
                if side == 0:
                    value = 6.0 * centre + line - bent
                else:
                    value = value + (6.0 * centre - line + bent)
            faces[i, begin : begin + 8, :] = value
        return carry

    lax.fori_loop(0, VARIABLES, upwind, 0)

    keep = wanted >= 0

    def back(index, carry):
        base = pl.multiple_of(index * 2 * GROUP, 2 * GROUP)
        high, low = [], []
        for v in range(VARIABLES):
            pieces = []
            for begin in (0, GROUP):
                here = faces[v, pl.ds(base + begin, GROUP), :]
                after = faces[v, pl.ds(base + begin + 1, GROUP), :]
                pieces.append(after - here)
            one, two = split(jnp.concatenate(pieces, axis=1))
            high.append(one)
            low.append(two)
        high = jnp.concatenate(high, axis=0)
        low = jnp.concatenate(low, axis=0)
        both = dot(right_high, high) + dot(right_high, low) + dot(right_low, high)
        both = both.reshape(VARIABLES, GROUP, 2 * slots)
        for part, begin in enumerate((0, GROUP)):
            piece = jnp.where(keep[None], both[:, :, part * slots : part * slots + slots], 0.0)
            one, two = split(piece)
            change_ref[:, pl.ds(base + begin, GROUP), :slots] = one
            change_ref[:, pl.ds(base + begin, GROUP), slots:] = two
        return carry

    lax.fori_loop(0, cells_z // (2 * GROUP), back, 0, unroll=True)


def shock(wanted, conserved, face, basis):
    _, cells_x, cells_y, cells_z = conserved.shape
    slots = wanted.shape[-1]
    total = cells_x * cells_y
    span = -(-(cells_z + 2 * LEAD) // GROUP) * GROUP
    vmem = pltpu.VMEM
    work = vmem((2, span + 8, slots), F32)
    scratch = [
        vmem((VARIABLES, slots, cells_z), F32),
        vmem((VARIABLES, span, slots), F32),
        vmem((span, slots), F32),
        vmem((span, slots), F32),
        vmem((VARIABLES, span + 8, slots), F32),
        vmem((VARIABLES, span + 8, slots), F32),
        work,
        work,
        work,
        work,
        work,
        vmem((VARIABLES, cells_z + 8, slots), F32),
        vmem((LANES, total), F32),
    ]
    smem = pl.BlockSpec(memory_space=pltpu.SMEM)
    whole = pl.BlockSpec(memory_space=pltpu.VMEM)
    return pl.pallas_call(
        shock_kernel,
        out_shape=[
            jax.ShapeDtypeStruct((VARIABLES, cells_z, 2 * slots), BF16),
            jax.ShapeDtypeStruct((total, 2 * slots), BF16),
            jax.ShapeDtypeStruct((total, LANES), F32),
            jax.ShapeDtypeStruct((4, total, cells_z), F32),
        ],
        in_specs=[smem, whole, whole, whole, whole],
        out_specs=[whole] * 4,
        scratch_shapes=scratch,
        compiler_params=pltpu.CompilerParams(vmem_limit_bytes=24 << 20),
        cost_estimate=pl.CostEstimate(flops=100_000_000, bytes_accessed=1_000_000, transcendentals=0),
        name="shock",
    )(wanted, wanted, conserved, face, basis)


def advance_kernel(
    u_ref, change_ref, hot_ref, edge_ref, state_ref, before_ref, after_ref, out_ref, done, left, right, rim, out_sem
):
    _, total, cells_z = u_ref.shape
    cells_x = before_ref.shape[2]
    cells_y = total // cells_x
    halves = cells_z // LANES
    scale = time_step / 60.0
    rows = right.shape[2] // 2 - cells_z

    row = lax.broadcasted_iota(jnp.int32, (cells_z, cells_z), 0)
    column = lax.broadcasted_iota(jnp.int32, (cells_z, cells_z), 1)
    along_z = stencil(row - column).astype(BF16)
    row = lax.broadcasted_iota(jnp.int32, (rows, rows), 0)
    column = lax.broadcasted_iota(jnp.int32, (rows, rows), 1)
    inside = row // cells_y == column // cells_y
    along_y = jnp.where(inside, stencil(column - row), 0.0).astype(BF16)
    for turn in range(2):
        for block in range(total // rows):
            for k in range(2):
                left[turn, block, :, 2 * cells_z + k * rows : 2 * cells_z + k * rows + rows] = along_y
                right[turn, block, k * cells_z : k * cells_z + cells_z, :] = along_z

    rim[...] = jnp.zeros_like(rim)
    for half in range(halves):
        wide = slice(half * LANES, half * LANES + LANES)
        f0, f1, f2 = (flux_of([before_ref[j, v, :, wide] for v in range(VARIABLES)], 1) for j in range(WIDTH))
        for v in range(VARIABLES):
            for j, part in enumerate((45.0 * f2[v] - 9.0 * f1[v] + f0[v], f1[v] - 9.0 * f2[v], f2[v])):
                rim[v, half, pl.ds(j, cells_x, stride=2 * GROUP), :] = scale * part
        f0, f1, f2 = (flux_of([after_ref[j, v, :, wide] for v in range(VARIABLES)], 1) for j in range(WIDTH))
        for v in range(VARIABLES):
            for j, part in enumerate((f0[v], f1[v] - 9.0 * f0[v], 45.0 * f0[v] - 9.0 * f1[v] + f2[v])):
                rim[v, half, pl.ds(2 * GROUP - WIDTH + j, cells_x, stride=2 * GROUP), :] = -scale * part

    lane = lax.broadcasted_iota(jnp.int32, (GROUP, LANES), 1)
    for v in range(VARIABLES):
        turn = v % 2

        for begin in range(0, total, GROUP):
            at = slice(begin, begin + GROUP)
            block, place = begin // rows, begin % rows
            value = u_ref[v, at, :]
            flux_y = value * state_ref[0, at, :]
            flux_z = value * state_ref[1, at, :]
            if v == SPECIES + 1:
                flux_y = flux_y + scale * state_ref[2, at, :]
            if v == SPECIES + 2:
                flux_z = flux_z + state_ref[3, at, :]
            if v == SPECIES + 3:
                flux_y = flux_y + state_ref[2, at, :] * state_ref[0, at, :]
                flux_z = flux_z + state_ref[2, at, :] * state_ref[1, at, :]
            high, low = split(flux_z)
            left[turn, block, place : place + GROUP, :cells_z] = high
            left[turn, block, place : place + GROUP, cells_z : 2 * cells_z] = low
            high, low = split(flux_y)
            place = place + 2 * cells_z
            right[turn, block, place : place + GROUP, :] = high
            right[turn, block, place + rows : place + rows + GROUP, :] = low
        for block in range(total // rows):
            base = block * rows
            gained = dot(left[turn, block], right[turn, block])
            gained = gained + lax.dot_general(
                hot_ref[base : base + rows, :], change_ref[v], (((1,), (1,)), ((), ())), preferred_element_type=F32
            )
            for begin in range(base, base + rows, GROUP):
                at = slice(begin, begin + GROUP)
                x, y = begin // cells_y, begin % cells_y
                border = pltpu.roll(edge_ref[at, :], (LANES - WIDTH - 8 * v) % LANES, 1)
                for half in range(halves):
                    wide = slice(half * LANES, half * LANES + LANES)
                    value = u_ref[v, at, wide] - gained[begin - base : begin - base + GROUP, wide]
                    if half == 0:
                        value = value - jnp.where(lane < WIDTH, border, 0.0)
                    if half == halves - 1:
                        value = value - jnp.where(lane >= LANES - WIDTH, border, 0.0)
                    if y == 0:
                        value = value + rim[v, half, 2 * GROUP * x : 2 * GROUP * x + GROUP, :]
                    if y == cells_y - GROUP:
                        value = value + rim[v, half, 2 * GROUP * x + GROUP : 2 * GROUP * x + 2 * GROUP, :]
                    done[v, at, wide] = value
        pltpu.make_async_copy(done.at[v], out_ref.at[v], out_sem).start()
    pltpu.make_async_copy(done, done, out_sem).wait()


def advance(conserved, change, hot, edge, state, before, after):
    _, cells_x, cells_y, cells_z = conserved.shape
    total = cells_x * cells_y
    rows = cells_y * max(1, min(cells_x, 256 // cells_y))
    whole = pl.BlockSpec(memory_space=pltpu.VMEM)
    result = pl.pallas_call(
        advance_kernel,
        out_shape=jax.ShapeDtypeStruct((VARIABLES, total, cells_z), F32),
        in_specs=[whole] * 7,
        out_specs=pl.BlockSpec(memory_space=pl.ANY),
        scratch_shapes=[
            pltpu.VMEM((VARIABLES, total, cells_z), F32),
            pltpu.VMEM((2, total // rows, rows, 2 * (cells_z + rows)), BF16),
            pltpu.VMEM((2, total // rows, 2 * (cells_z + rows), cells_z), BF16),
            pltpu.VMEM((VARIABLES, cells_z // LANES, cells_x * 2 * GROUP, LANES), F32),
            pltpu.SemaphoreType.DMA(()),
        ],
        compiler_params=pltpu.CompilerParams(vmem_limit_bytes=24 << 20),
        cost_estimate=pl.CostEstimate(flops=4_000_000_000, bytes_accessed=20_000_000, transcendentals=0),
        name="advance",
    )(conserved.reshape(VARIABLES, total, cells_z), change, hot, edge, state, before, after)
    return result.reshape(conserved.shape)


def on_device(conserved, char_left, char_right, shock_list, shock_count):
    count = lax.axis_size("gy")
    ahead = [(i, (i + 1) % count) for i in range(count)]
    tail, head, first = pack_y(conserved)
    before = lax.ppermute(tail, "gy", ahead)
    after = lax.ppermute(head, "gy", [(b, a) for a, b in ahead])
    basis = jnp.stack([0.5 * char_left, (time_step / 3.0) * char_right])
    slots = shock_list.shape[-1]
    wanted = jnp.where(jnp.arange(slots, dtype=jnp.int32) < shock_count, shock_list, -1).reshape(1, slots)
    face = exchange_z(pack_z(conserved, first, basis, wanted))
    change, hot, edge, state = shock(
        wanted, conserved, face, basis
    )
    return advance(conserved, change, hot, edge, state, before, after)


def solution(mesh):
    placed = (P(None, "gx", "gy", "gz"), P(), P(), P("gx", "gy", "gz", None), P("gx", "gy", "gz"))
    return jax.shard_map(
        on_device, mesh=mesh, in_specs=placed, out_specs=P(None, "gx", "gy", "gz"), check_vma=False
    )
```

```python
import functools

import jax
import jax.numpy as jnp
from jax import lax
from jax.experimental import pallas as pl
from jax.experimental.pallas import tpu as pltpu
from jax.sharding import PartitionSpec as P

SPECIES = 9
VARIABLES = 14
WIDTH = 3
GROUP = 16
LANES = 128
LEAD = 8

gas_excess = 0.4
time_step = 0.2
weno_epsilon = 1e-06

F32 = jnp.float32
BF16 = jnp.bfloat16


def split(values):
    high = values.astype(BF16)
    low = (values - high.astype(F32)).astype(BF16)
    return high, low


def dot(left, right):
    return jnp.dot(left, right, preferred_element_type=F32)


def state_of(parts):
    density = parts[0]
    for index in range(1, SPECIES):
        density = density + parts[index]
    inverse = pl.reciprocal(density, approx=True)
    first, second, last = parts[SPECIES], parts[SPECIES + 1], parts[SPECIES + 2]
    kinetic = 0.5 * (first * first + second * second + last * last) * inverse
    pressure = gas_excess * (parts[SPECIES + 3] - parts[SPECIES + 4] - kinetic)
    return inverse, pressure


def flux_of(parts, normal):
    inverse, pressure = state_of(parts)
    velocity = parts[SPECIES + normal] * inverse
    result = [part * velocity for part in parts]
    result[SPECIES + normal] = result[SPECIES + normal] + pressure
    result[SPECIES + 3] = result[SPECIES + 3] + pressure * velocity
    return result


def pack_y_kernel(u_ref, tail_ref, head_ref, first_ref, sem):
    cells_x, cells_y = u_ref.shape[1], u_ref.shape[2]
    for x in range(cells_x):
        for j in range(WIDTH):
            pltpu.make_async_copy(
                u_ref.at[:, x, pl.ds(cells_y - WIDTH + j, 1), :], tail_ref.at[j, :, pl.ds(x, 1), :], sem
            ).start()
            pltpu.make_async_copy(
                u_ref.at[:, x, pl.ds(j, 1), :], head_ref.at[j, :, pl.ds(x, 1), :], sem
            ).start()
    first_ref[...] = jnp.zeros_like(first_ref)
    pltpu.make_async_copy(tail_ref, tail_ref, sem).wait()
    pltpu.make_async_copy(head_ref, head_ref, sem).wait()


def pack_y(conserved):
    cells_x, cells_z = conserved.shape[1], conserved.shape[3]
    face = jax.ShapeDtypeStruct((WIDTH, VARIABLES, cells_x, cells_z), F32)
    return pl.pallas_call(
        pack_y_kernel,
        out_shape=[face, face, jax.ShapeDtypeStruct((8, LANES), F32)],
        in_specs=[pl.BlockSpec(memory_space=pl.ANY)],
        out_specs=[pl.BlockSpec(memory_space=pltpu.VMEM)] * 3,
        scratch_shapes=[pltpu.SemaphoreType.DMA(())],
        compiler_params=pltpu.CompilerParams(vmem_limit_bytes=16 << 20),
        cost_estimate=pl.CostEstimate(flops=0, bytes_accessed=2_000_000, transcendentals=0),
        name="pack_y",
    )(conserved)


def pack_z_kernel(u_ref, first_ref, basis_ref, wanted_ref, face_ref):
    _, cells_x, cells_y, cells_z = u_ref.shape
    lane = lax.broadcasted_iota(jnp.int32, (cells_y, LANES), 1)
    for x in range(cells_x):
        packed = jnp.zeros((cells_y, LANES), F32)
        for v in range(VARIABLES):
            both = jnp.where(lane < LANES // 2, u_ref[v, x, :, :LANES], u_ref[v, x, :, cells_z - LANES :])
            packed = jnp.where(lane >> 3 == v, pltpu.roll(both, 8 * v + WIDTH, 1), packed)
        face_ref[x * cells_y : (x + 1) * cells_y, :] = packed


def pack_z(conserved, first, basis, wanted):
    _, cells_x, cells_y, _ = conserved.shape
    whole = pl.BlockSpec(memory_space=pltpu.VMEM)
    return pl.pallas_call(
        pack_z_kernel,
        out_shape=jax.ShapeDtypeStruct((cells_x * cells_y, LANES), F32),
        in_specs=[whole] * 4,
        out_specs=whole,
        compiler_params=pltpu.CompilerParams(vmem_limit_bytes=16 << 20),
        cost_estimate=pl.CostEstimate(flops=4_000_000, bytes_accessed=9_000_000, transcendentals=0),
        name="pack_z",
    )(conserved, first, basis, wanted)


def exchange_z(packed):
    count = lax.axis_size("gz")
    if count == 1:
        return packed
    ahead = [(i, (i + 1) % count) for i in range(count)]
    from_left = lax.ppermute(packed, "gz", ahead)
    if count == 2:
        return from_left
    from_right = lax.ppermute(packed, "gz", [(b, a) for a, b in ahead])
    lane = jnp.arange(LANES, dtype=jnp.int32)[None, :]
    return jnp.where(lane & 7 < WIDTH, from_left, from_right)


def spread_matrix(matrix):
    rows = VARIABLES * GROUP
    pick = lax.broadcasted_iota(jnp.int32, (rows, VARIABLES), 0) >> 4
    pick = (pick == lax.broadcasted_iota(jnp.int32, (rows, VARIABLES), 1)).astype(F32)
    tall = jnp.dot(pick, matrix, precision=lax.Precision.HIGHEST, preferred_element_type=F32)
    wide = lax.dot_general(
        tall, pick, (((1,), (1,)), ((), ())), precision=lax.Precision.HIGHEST, preferred_element_type=F32
    )
    row = lax.broadcasted_iota(jnp.int32, (rows, rows), 0) & (GROUP - 1)
    column = lax.broadcasted_iota(jnp.int32, (rows, rows), 1) & (GROUP - 1)
    return split(jnp.where(row == column, wide, 0.0))


def stencil(offset):
    size = jnp.abs(offset)
    weight = jnp.where(size == 1, 45.0, jnp.where(size == 2, -9.0, jnp.where(size == 3, 1.0, 0.0)))
    return jnp.where(offset < 0, -weight, weight)


def prepare_kernel(list_ref, wanted_ref, u_ref, face_ref, state_ref, pencils):
    _, cells_x, cells_y, cells_z = u_ref.shape
    slots = wanted_ref.shape[-1]
    total = cells_x * cells_y
    scale = time_step / 60.0
    wanted = wanted_ref[...]

    def fetch(p):
        place = jnp.maximum(list_ref[0, p], 0)
        x, y = place // cells_y, place % cells_y
        for v in range(VARIABLES):
            pencils[v, pl.ds(p, 1), :] = u_ref[v, x, pl.ds(y, 1), :]

    def state(index, carry):
        at = slice(index * 8, index * 8 + 8)
        x, y = index * 8 // cells_y, index * 8 % cells_y
        pencil = index * 8 + lax.broadcasted_iota(jnp.int32, (8, slots), 0)
        calm = scale - scale * jnp.sum((wanted == pencil).astype(F32), axis=1, keepdims=True)
        for begin in range(0, cells_z, LANES):
            wide = slice(begin, begin + LANES)
            parts = [u_ref[v, x, y : y + 8, wide] for v in range(VARIABLES)]
            inverse, pressure = state_of(parts)
            state_ref[0, at, wide] = parts[SPECIES + 1] * (inverse * scale)
            state_ref[1, at, wide] = parts[SPECIES + 2] * (inverse * calm)
            state_ref[2, at, wide] = pressure
            state_ref[3, at, wide] = pressure * calm
        return carry

    for index in range(total // 8):
        state(index, 0)
        for p in range(index * 8 * slots // total, (index + 1) * 8 * slots // total):
            fetch(p)


def prepare(wanted, conserved, packed):
    _, cells_x, cells_y, cells_z = conserved.shape
    slots = wanted.shape[-1]
    whole = pl.BlockSpec(memory_space=pltpu.VMEM)
    return pl.pallas_call(
        prepare_kernel,
        out_shape=[
            jax.ShapeDtypeStruct((4, cells_x * cells_y, cells_z), F32),
            jax.ShapeDtypeStruct((VARIABLES, slots, cells_z), F32),
        ],
        in_specs=[pl.BlockSpec(memory_space=pltpu.SMEM), whole, whole, whole],
        out_specs=[whole] * 2,
        compiler_params=pltpu.CompilerParams(vmem_limit_bytes=16 << 20),
        cost_estimate=pl.CostEstimate(flops=8_000_000, bytes_accessed=9_000_000, transcendentals=0),
        name="prepare",
    )(wanted, wanted, conserved, packed)


def shock_kernel(
    list_ref,
    wanted_ref,
    pencils,
    face_ref,
    basis_ref,
    change_ref,
    hot_ref,
    edge_ref,
    turned,
    speed_t,
    press_t,
    g_out,
    g_in,
    delta,
    triple,
    smooth,
    curve,
    third,
    faces,
    edge_t,
):
    slots = wanted_ref.shape[-1]
    total = face_ref.shape[0]
    cells_z = pencils.shape[2]
    span = turned.shape[1]


    wanted = wanted_ref[...]
    scale = time_step / 60.0

    for begin in range(0, total, LANES):
        edge_t[:, begin : begin + LANES] = face_ref[begin : begin + LANES, :].T
    fluxes = flux_of([edge_t[8 * v : 8 * v + 8, :] for v in range(VARIABLES)], 2)
    for v in range(VARIABLES):
        edge_t[8 * v : 8 * v + 8, :] = fluxes[v]
    row = lax.broadcasted_iota(jnp.int32, (LANES, LANES), 0)
    column = lax.broadcasted_iota(jnp.int32, (LANES, LANES), 1)
    target, source = row & 7, column & 7
    reach = jnp.logical_xor(target < WIDTH, source < WIDTH)
    reach = reach & (target < 2 * WIDTH) & (source < 2 * WIDTH) & (row >> 3 == column >> 3)
    weights = jnp.where(reach, stencil(source - target), 0.0).astype(BF16)
    for begin in range(0, total, LANES):
        wide = slice(begin, begin + LANES)
        high, low = split(edge_t[:, wide])
        pencil = begin + lax.broadcasted_iota(jnp.int32, (LANES, slots), 0)
        hot = (wanted == pencil).astype(F32)
        calm = scale - scale * jnp.sum(hot, axis=1, keepdims=True)
        edge_ref[wide, :] = (dot(weights, high) + dot(weights, low)).T * calm
        hot = hot.astype(BF16)
        hot_ref[wide, :slots] = hot
        hot_ref[wide, slots:] = hot

    left_high, left_low = spread_matrix(basis_ref[0])
    right_high, right_low = spread_matrix(basis_ref[1])

    def neighbour(p, carry):
        speed_t[pl.ds(p, 1), :] = face_ref[pl.ds(jnp.maximum(list_ref[0, p], 0), 1), :]
        return carry

    lax.fori_loop(0, slots, neighbour, 0, unroll=8)
    border = speed_t[0:slots, :].T

    for v in range(VARIABLES):
        tile = border[8 * v : 8 * v + 8, :]
        turned[v, 0:LEAD, :] = tile
        turned[v, span - 8 : span, :] = tile
        turned[v, LEAD - WIDTH : LEAD - WIDTH + 8, :] = tile
        turned[v, LEAD + cells_z - WIDTH : LEAD + cells_z - WIDTH + 8, :] = tile
        for begin in range(0, cells_z, LANES):
            turned[v, LEAD + begin : LEAD + begin + LANES, :] = pencils[v, :, begin : begin + LANES].T

    top = jnp.zeros((8, slots), F32)
    for begin in range(0, span, 8):
        parts = [turned[v, begin : begin + 8, :] for v in range(VARIABLES)]
        inverse, pressure = state_of(parts)
        velocity = parts[SPECIES + 2] * inverse
        speed_t[begin : begin + 8, :] = 0.5 * velocity
        press_t[begin : begin + 8, :] = pressure
        size = jnp.abs(velocity)
        if begin < LEAD - WIDTH or begin + 8 > LEAD + cells_z + WIDTH:
            at = begin + lax.broadcasted_iota(jnp.int32, (8, slots), 0)
            size = jnp.where((at >= LEAD - WIDTH) & (at < LEAD + cells_z + WIDTH), size, 0.0)
        top = jnp.maximum(top, size)
    wave = 0.5 * (jnp.max(top, axis=0, keepdims=True) + 1.0)

    def project(index, carry):
        at = pl.ds(pl.multiple_of(index * GROUP, GROUP), GROUP)
        velocity = speed_t[at, :]
        pressure = press_t[at, :]
        parts = [turned[v, at, :] for v in range(VARIABLES)]
        flux = [part * velocity for part in parts]
        flux[SPECIES + 2] = flux[SPECIES + 2] + 0.5 * pressure
        flux[SPECIES + 3] = flux[SPECIES + 3] + pressure * velocity
        high, low = [], []
        for v in range(VARIABLES):
            one, two = split(jnp.concatenate([flux[v], wave * parts[v]], axis=1))
            high.append(one)
            low.append(two)
        high = jnp.concatenate(high, axis=0)
        low = jnp.concatenate(low, axis=0)
        both = dot(left_high, high) + dot(left_high, low) + dot(left_low, high)
        both = both.reshape(VARIABLES, GROUP, 2 * slots)
        g_out[:, at, :] = both[:, :, :slots] + both[:, :, slots:]
        g_in[:, at, :] = both[:, :, :slots] - both[:, :, slots:]
        return carry

    lax.fori_loop(0, span // GROUP, project, 0, unroll=True)

    def upwind(i, carry):
        for side, source in enumerate((g_out, g_in)):
            for begin in range(0, span, 8):
                step = source[i, begin + 1 : begin + 9, :] - source[i, begin : begin + 8, :]
                delta[side, begin : begin + 8, :] = step
                triple[side, begin : begin + 8, :] = 3.0 * step
            for begin in range(1, span, 8):
                bend = delta[side, begin : begin + 8, :] - delta[side, begin - 1 : begin + 7, :]
                curve[side, begin : begin + 8, :] = bend
                smooth[side, begin : begin + 8, :] = (13.0 / 3.0 * bend) * bend + weno_epsilon
            for begin in range(0, span, 8):
                third[side, begin : begin + 8, :] = (
                    curve[side, begin + 1 : begin + 9, :] - curve[side, begin : begin + 8, :]
                )
        for begin in range(0, cells_z + 8, 8):
            at = begin + LEAD - 1

            def read(ref, side, offset):
                return ref[side, at + offset : at + offset + 8, :]

            value = None
            for side, source in enumerate((g_out, g_in)):
                if side == 0:
                    d1, d2, d3, d4 = (read(delta, 0, o) for o in (-2, -1, 0, 1))
                    three2, three3 = read(triple, 0, -1), read(triple, 0, 0)
                    s1, s2, s3 = (read(smooth, 0, o) for o in (-1, 0, 1))
                    u1, u2 = (read(third, 0, o) for o in (-1, 0))
                else:
                    d1, d2, d3, d4 = (read(delta, 1, o) for o in (2, 1, 0, -1))
                    three2, three3 = read(triple, 1, 1), read(triple, 1, 0)
                    s1, s2, s3 = (read(smooth, 1, o) for o in (2, 1, 0))
                    u1, u2 = (read(third, 1, o) for o in (1, 0))
                centre = source[i, at + side : at + side + 8, :]
                t0 = three2 - d1
                t1 = d2 + d3
                t2 = d4 - three3
                r0 = pl.reciprocal(s1 + t0 * t0, approx=True)
                r1 = pl.reciprocal(s2 + t1 * t1, approx=True)
                r2 = pl.reciprocal(s3 + t2 * t2, approx=True)
                w0 = r0 * (r0 * (1.0 / 3.0))
                w1 = r1 * r1
                w2 = r2 * r2
                above = (w0 + w0) * u1 + w2 * u2
                below = (w0 + w2) + (w1 + w1)
                bent = above * pl.reciprocal(below, approx=True)
                line = t1 + d3
                if side == 0:
                    value = 6.0 * centre + line - bent
                else:
                    value = value + (6.0 * centre - line + bent)
            faces[i, begin : begin + 8, :] = value
        return carry

    lax.fori_loop(0, VARIABLES, upwind, 0)

    keep = wanted >= 0

    def back(index, carry):
        base = pl.multiple_of(index * 2 * GROUP, 2 * GROUP)
        high, low = [], []
        for v in range(VARIABLES):
            pieces = []
            for begin in (0, GROUP):
                here = faces[v, pl.ds(base + begin, GROUP), :]
                after = faces[v, pl.ds(base + begin + 1, GROUP), :]
                pieces.append(after - here)
            one, two = split(jnp.concatenate(pieces, axis=1))
            high.append(one)
            low.append(two)
        high = jnp.concatenate(high, axis=0)
        low = jnp.concatenate(low, axis=0)
        both = dot(right_high, high) + dot(right_high, low) + dot(right_low, high)
        both = both.reshape(VARIABLES, GROUP, 2 * slots)
        for part, begin in enumerate((0, GROUP)):
            piece = jnp.where(keep[None], both[:, :, part * slots : part * slots + slots], 0.0)
            one, two = split(piece)
            change_ref[:, pl.ds(base + begin, GROUP), :slots] = one
            change_ref[:, pl.ds(base + begin, GROUP), slots:] = two
        return carry

    lax.fori_loop(0, cells_z // (2 * GROUP), back, 0, unroll=True)


def shock(wanted, pencils, face, basis):
    cells_z = pencils.shape[2]
    slots = wanted.shape[-1]
    total = face.shape[0]
    span = -(-(cells_z + 2 * LEAD) // GROUP) * GROUP
    vmem = pltpu.VMEM
    work = vmem((2, span + 8, slots), F32)
    scratch = [
        vmem((VARIABLES, span, slots), F32),
        vmem((span, slots), F32),
        vmem((span, slots), F32),
        vmem((VARIABLES, span + 8, slots), F32),
        vmem((VARIABLES, span + 8, slots), F32),
        work,
        work,
        work,
        work,
        work,
        vmem((VARIABLES, cells_z + 8, slots), F32),
        vmem((LANES, total), F32),
    ]
    smem = pl.BlockSpec(memory_space=pltpu.SMEM)
    whole = pl.BlockSpec(memory_space=pltpu.VMEM)
    return pl.pallas_call(
        shock_kernel,
        out_shape=[
            jax.ShapeDtypeStruct((VARIABLES, cells_z, 2 * slots), BF16),
            jax.ShapeDtypeStruct((total, 2 * slots), BF16),
            jax.ShapeDtypeStruct((total, LANES), F32),
        ],
        in_specs=[smem, whole, whole, whole, whole],
        out_specs=[whole] * 3,
        scratch_shapes=scratch,
        compiler_params=pltpu.CompilerParams(vmem_limit_bytes=24 << 20),
        cost_estimate=pl.CostEstimate(flops=100_000_000, bytes_accessed=1_000_000, transcendentals=0),
        name="shock",
    )(wanted, wanted, pencils, face, basis)


def advance_kernel(
    u_ref, change_ref, hot_ref, edge_ref, state_ref, before_ref, after_ref, out_ref, done, left, right, rim, out_sem
):
    _, total, cells_z = u_ref.shape
    cells_x = before_ref.shape[2]
    cells_y = total // cells_x
    halves = cells_z // LANES
    scale = time_step / 60.0
    rows = right.shape[2] // 2 - cells_z

    row = lax.broadcasted_iota(jnp.int32, (cells_z, cells_z), 0)
    column = lax.broadcasted_iota(jnp.int32, (cells_z, cells_z), 1)
    along_z = stencil(row - column).astype(BF16)
    row = lax.broadcasted_iota(jnp.int32, (rows, rows), 0)
    column = lax.broadcasted_iota(jnp.int32, (rows, rows), 1)
    inside = row // cells_y == column // cells_y
    along_y = jnp.where(inside, stencil(column - row), 0.0).astype(BF16)
    for turn in range(2):
        for block in range(total // rows):
            for k in range(2):
                left[turn, block, :, 2 * cells_z + k * rows : 2 * cells_z + k * rows + rows] = along_y
                right[turn, block, k * cells_z : k * cells_z + cells_z, :] = along_z

    rim[...] = jnp.zeros_like(rim)
    for half in range(halves):
        wide = slice(half * LANES, half * LANES + LANES)
        f0, f1, f2 = (flux_of([before_ref[j, v, :, wide] for v in range(VARIABLES)], 1) for j in range(WIDTH))
        for v in range(VARIABLES):
            for j, part in enumerate((45.0 * f2[v] - 9.0 * f1[v] + f0[v], f1[v] - 9.0 * f2[v], f2[v])):
                rim[v, half, pl.ds(j, cells_x, stride=2 * GROUP), :] = scale * part
        f0, f1, f2 = (flux_of([after_ref[j, v, :, wide] for v in range(VARIABLES)], 1) for j in range(WIDTH))
        for v in range(VARIABLES):
            for j, part in enumerate((f0[v], f1[v] - 9.0 * f0[v], 45.0 * f0[v] - 9.0 * f1[v] + f2[v])):
                rim[v, half, pl.ds(2 * GROUP - WIDTH + j, cells_x, stride=2 * GROUP), :] = -scale * part

    lane = lax.broadcasted_iota(jnp.int32, (GROUP, LANES), 1)
    for v in range(VARIABLES):
        turn = v % 2

        for begin in range(0, total, GROUP):
            at = slice(begin, begin + GROUP)
            block, place = begin // rows, begin % rows
            value = u_ref[v, at, :]
            flux_y = value * state_ref[0, at, :]
            flux_z = value * state_ref[1, at, :]
            if v == SPECIES + 1:
                flux_y = flux_y + scale * state_ref[2, at, :]
            if v == SPECIES + 2:
                flux_z = flux_z + state_ref[3, at, :]
            if v == SPECIES + 3:
                flux_y = flux_y + state_ref[2, at, :] * state_ref[0, at, :]
                flux_z = flux_z + state_ref[2, at, :] * state_ref[1, at, :]
            high, low = split(flux_z)
            left[turn, block, place : place + GROUP, :cells_z] = high
            left[turn, block, place : place + GROUP, cells_z : 2 * cells_z] = low
            high, low = split(flux_y)
            place = place + 2 * cells_z
            right[turn, block, place : place + GROUP, :] = high
            right[turn, block, place + rows : place + rows + GROUP, :] = low
        for block in range(total // rows):
            base = block * rows
            gained = dot(left[turn, block], right[turn, block])
            gained = gained + lax.dot_general(
                hot_ref[base : base + rows, :], change_ref[v], (((1,), (1,)), ((), ())), preferred_element_type=F32
            )
            for begin in range(base, base + rows, GROUP):
                at = slice(begin, begin + GROUP)
                x, y = begin // cells_y, begin % cells_y
                border = pltpu.roll(edge_ref[at, :], (LANES - WIDTH - 8 * v) % LANES, 1)
                for half in range(halves):
                    wide = slice(half * LANES, half * LANES + LANES)
                    value = u_ref[v, at, wide] - gained[begin - base : begin - base + GROUP, wide]
                    if half == 0:
                        value = value - jnp.where(lane < WIDTH, border, 0.0)
                    if half == halves - 1:
                        value = value - jnp.where(lane >= LANES - WIDTH, border, 0.0)
                    if y == 0:
                        value = value + rim[v, half, 2 * GROUP * x : 2 * GROUP * x + GROUP, :]
                    if y == cells_y - GROUP:
                        value = value + rim[v, half, 2 * GROUP * x + GROUP : 2 * GROUP * x + 2 * GROUP, :]
                    done[v, at, wide] = value
        pltpu.make_async_copy(done.at[v], out_ref.at[v], out_sem).start()
    pltpu.make_async_copy(done, done, out_sem).wait()


def advance(conserved, change, hot, edge, state, before, after):
    _, cells_x, cells_y, cells_z = conserved.shape
    total = cells_x * cells_y
    rows = cells_y * max(1, min(cells_x, 256 // cells_y))
    whole = pl.BlockSpec(memory_space=pltpu.VMEM)
    result = pl.pallas_call(
        advance_kernel,
        out_shape=jax.ShapeDtypeStruct((VARIABLES, total, cells_z), F32),
        in_specs=[whole] * 7,
        out_specs=pl.BlockSpec(memory_space=pl.ANY),
        scratch_shapes=[
            pltpu.VMEM((VARIABLES, total, cells_z), F32),
            pltpu.VMEM((2, total // rows, rows, 2 * (cells_z + rows)), BF16),
            pltpu.VMEM((2, total // rows, 2 * (cells_z + rows), cells_z), BF16),
            pltpu.VMEM((VARIABLES, cells_z // LANES, cells_x * 2 * GROUP, LANES), F32),
            pltpu.SemaphoreType.DMA(()),
        ],
        compiler_params=pltpu.CompilerParams(vmem_limit_bytes=24 << 20),
        cost_estimate=pl.CostEstimate(flops=4_000_000_000, bytes_accessed=20_000_000, transcendentals=0),
        name="advance",
    )(conserved.reshape(VARIABLES, total, cells_z), change, hot, edge, state, before, after)
    return result.reshape(conserved.shape)


def on_device(conserved, char_left, char_right, shock_list, shock_count):
    count = lax.axis_size("gy")
    ahead = [(i, (i + 1) % count) for i in range(count)]
    tail, head, first = pack_y(conserved)
    before = lax.ppermute(tail, "gy", ahead)
    after = lax.ppermute(head, "gy", [(b, a) for a, b in ahead])
    basis = jnp.stack([0.5 * char_left, (time_step / 3.0) * char_right])
    slots = shock_list.shape[-1]
    wanted = jnp.where(jnp.arange(slots, dtype=jnp.int32) < shock_count, shock_list, -1).reshape(1, slots)
    packed = pack_z(conserved, first, basis, wanted)
    face = exchange_z(packed)
    state, pencils = prepare(wanted, conserved, packed)
    change, hot, edge = shock(wanted, pencils, face, basis)
    return advance(conserved, change, hot, edge, state, before, after)


def solution(mesh):
    placed = (P(None, "gx", "gy", "gz"), P(), P(), P("gx", "gy", "gz", None), P("gx", "gy", "gz"))
    return jax.shard_map(
        on_device, mesh=mesh, in_specs=placed, out_specs=P(None, "gx", "gy", "gz"), check_vma=False
    )
```

```python
import functools

import jax
import jax.numpy as jnp
from jax import lax
from jax.experimental import pallas as pl
from jax.experimental.pallas import tpu as pltpu
from jax.sharding import PartitionSpec as P

SPECIES = 9
VARIABLES = 14
WIDTH = 3
GROUP = 16
LANES = 128
LEAD = 8

gas_excess = 0.4
time_step = 0.2
weno_epsilon = 1e-06

F32 = jnp.float32
BF16 = jnp.bfloat16


def split(values):
    high = values.astype(BF16)
    low = (values - high.astype(F32)).astype(BF16)
    return high, low


def dot(left, right):
    return jnp.dot(left, right, preferred_element_type=F32)


def state_of(parts):
    density = parts[0]
    for index in range(1, SPECIES):
        density = density + parts[index]
    inverse = pl.reciprocal(density, approx=True)
    first, second, last = parts[SPECIES], parts[SPECIES + 1], parts[SPECIES + 2]
    kinetic = 0.5 * (first * first + second * second + last * last) * inverse
    pressure = gas_excess * (parts[SPECIES + 3] - parts[SPECIES + 4] - kinetic)
    return inverse, pressure


def flux_of(parts, normal):
    inverse, pressure = state_of(parts)
    velocity = parts[SPECIES + normal] * inverse
    result = [part * velocity for part in parts]
    result[SPECIES + normal] = result[SPECIES + normal] + pressure
    result[SPECIES + 3] = result[SPECIES + 3] + pressure * velocity
    return result


def pack_y_kernel(u_ref, tail_ref, head_ref, first_ref, sem):
    cells_x, cells_y = u_ref.shape[1], u_ref.shape[2]
    for x in range(cells_x):
        for j in range(WIDTH):
            pltpu.make_async_copy(
                u_ref.at[:, x, pl.ds(cells_y - WIDTH + j, 1), :], tail_ref.at[j, :, pl.ds(x, 1), :], sem
            ).start()
            pltpu.make_async_copy(
                u_ref.at[:, x, pl.ds(j, 1), :], head_ref.at[j, :, pl.ds(x, 1), :], sem
            ).start()
    first_ref[...] = jnp.zeros_like(first_ref)
    pltpu.make_async_copy(tail_ref, tail_ref, sem).wait()
    pltpu.make_async_copy(head_ref, head_ref, sem).wait()


def pack_y(conserved):
    cells_x, cells_z = conserved.shape[1], conserved.shape[3]
    face = jax.ShapeDtypeStruct((WIDTH, VARIABLES, cells_x, cells_z), F32)
    return pl.pallas_call(
        pack_y_kernel,
        out_shape=[face, face, jax.ShapeDtypeStruct((8, LANES), F32)],
        in_specs=[pl.BlockSpec(memory_space=pl.ANY)],
        out_specs=[pl.BlockSpec(memory_space=pltpu.VMEM)] * 3,
        scratch_shapes=[pltpu.SemaphoreType.DMA(())],
        compiler_params=pltpu.CompilerParams(vmem_limit_bytes=16 << 20),
        cost_estimate=pl.CostEstimate(flops=0, bytes_accessed=2_000_000, transcendentals=0),
        name="pack_y",
    )(conserved)


def pack_z_kernel(u_ref, first_ref, basis_ref, wanted_ref, face_ref):
    _, cells_x, cells_y, cells_z = u_ref.shape
    lane = lax.broadcasted_iota(jnp.int32, (cells_y, LANES), 1)
    for x in range(cells_x):
        packed = jnp.zeros((cells_y, LANES), F32)
        for v in range(VARIABLES):
            both = jnp.where(lane < LANES // 2, u_ref[v, x, :, :LANES], u_ref[v, x, :, cells_z - LANES :])
            packed = jnp.where(lane >> 3 == v, pltpu.roll(both, 8 * v + WIDTH, 1), packed)
        face_ref[x * cells_y : (x + 1) * cells_y, :] = packed


def pack_z(conserved, first, basis, wanted):
    _, cells_x, cells_y, _ = conserved.shape
    whole = pl.BlockSpec(memory_space=pltpu.VMEM)
    return pl.pallas_call(
        pack_z_kernel,
        out_shape=jax.ShapeDtypeStruct((cells_x * cells_y, LANES), F32),
        in_specs=[whole] * 4,
        out_specs=whole,
        compiler_params=pltpu.CompilerParams(vmem_limit_bytes=16 << 20),
        cost_estimate=pl.CostEstimate(flops=4_000_000, bytes_accessed=9_000_000, transcendentals=0),
        name="pack_z",
    )(conserved, first, basis, wanted)


def exchange_z(packed):
    count = lax.axis_size("gz")
    if count == 1:
        return packed
    ahead = [(i, (i + 1) % count) for i in range(count)]
    from_left = lax.ppermute(packed, "gz", ahead)
    if count == 2:
        return from_left
    from_right = lax.ppermute(packed, "gz", [(b, a) for a, b in ahead])
    lane = jnp.arange(LANES, dtype=jnp.int32)[None, :]
    return jnp.where(lane & 7 < WIDTH, from_left, from_right)


def spread_matrix(matrix):
    rows = VARIABLES * GROUP
    pick = lax.broadcasted_iota(jnp.int32, (rows, VARIABLES), 0) >> 4
    pick = (pick == lax.broadcasted_iota(jnp.int32, (rows, VARIABLES), 1)).astype(F32)
    tall = jnp.dot(pick, matrix, precision=lax.Precision.HIGHEST, preferred_element_type=F32)
    wide = lax.dot_general(
        tall, pick, (((1,), (1,)), ((), ())), precision=lax.Precision.HIGHEST, preferred_element_type=F32
    )
    row = lax.broadcasted_iota(jnp.int32, (rows, rows), 0) & (GROUP - 1)
    column = lax.broadcasted_iota(jnp.int32, (rows, rows), 1) & (GROUP - 1)
    return split(jnp.where(row == column, wide, 0.0))


def stencil(offset):
    size = jnp.abs(offset)
    weight = jnp.where(size == 1, 45.0, jnp.where(size == 2, -9.0, jnp.where(size == 3, 1.0, 0.0)))
    return jnp.where(offset < 0, -weight, weight)


def shock_kernel(
    list_ref,
    wanted_ref,
    u_ref,
    face_ref,
    basis_ref,
    change_ref,
    hot_ref,
    edge_ref,
    state_ref,
    pencils,
    turned,
    speed_t,
    press_t,
    g_out,
    g_in,
    delta,
    triple,
    smooth,
    curve,
    third,
    faces,
    edge_t,
):
    _, cells_x, cells_y, cells_z = u_ref.shape
    slots = wanted_ref.shape[-1]
    total = cells_x * cells_y
    span = turned.shape[1]

    def fetch(p):
        place = jnp.maximum(list_ref[0, p], 0)
        x, y = place // cells_y, place % cells_y
        for v in range(VARIABLES):
            pencils[v, pl.ds(p, 1), :] = u_ref[v, x, pl.ds(y, 1), :]


    wanted = wanted_ref[...]
    scale = time_step / 60.0

    for begin in range(0, total, LANES):
        edge_t[:, begin : begin + LANES] = face_ref[begin : begin + LANES, :].T
    fluxes = flux_of([edge_t[8 * v : 8 * v + 8, :] for v in range(VARIABLES)], 2)
    for v in range(VARIABLES):
        edge_t[8 * v : 8 * v + 8, :] = fluxes[v]
    row = lax.broadcasted_iota(jnp.int32, (LANES, LANES), 0)
    column = lax.broadcasted_iota(jnp.int32, (LANES, LANES), 1)
    target, source = row & 7, column & 7
    reach = jnp.logical_xor(target < WIDTH, source < WIDTH)
    reach = reach & (target < 2 * WIDTH) & (source < 2 * WIDTH) & (row >> 3 == column >> 3)
    weights = jnp.where(reach, stencil(source - target), 0.0).astype(BF16)
    for begin in range(0, total, LANES):
        wide = slice(begin, begin + LANES)
        high, low = split(edge_t[:, wide])
        pencil = begin + lax.broadcasted_iota(jnp.int32, (LANES, slots), 0)
        hot = (wanted == pencil).astype(F32)
        calm = scale - scale * jnp.sum(hot, axis=1, keepdims=True)
        edge_ref[wide, :] = (dot(weights, high) + dot(weights, low)).T * calm
        hot = hot.astype(BF16)
        hot_ref[wide, :slots] = hot
        hot_ref[wide, slots:] = hot

    left_high, left_low = spread_matrix(basis_ref[0])
    right_high, right_low = spread_matrix(basis_ref[1])

    def neighbour(p, carry):
        speed_t[pl.ds(p, 1), :] = face_ref[pl.ds(jnp.maximum(list_ref[0, p], 0), 1), :]
        return carry

    lax.fori_loop(0, slots, neighbour, 0, unroll=8)
    border = speed_t[0:slots, :].T

    def state(index, carry):
        at = slice(index * 8, index * 8 + 8)
        x, y = index * 8 // cells_y, index * 8 % cells_y
        pencil = index * 8 + lax.broadcasted_iota(jnp.int32, (8, slots), 0)
        calm = scale - scale * jnp.sum((wanted == pencil).astype(F32), axis=1, keepdims=True)
        for begin in range(0, cells_z, LANES):
            wide = slice(begin, begin + LANES)
            parts = [u_ref[v, x, y : y + 8, wide] for v in range(VARIABLES)]
            inverse, pressure = state_of(parts)
            state_ref[0, at, wide] = parts[SPECIES + 1] * (inverse * scale)
            state_ref[1, at, wide] = parts[SPECIES + 2] * (inverse * calm)
            state_ref[2, at, wide] = pressure
            state_ref[3, at, wide] = pressure * calm
        return carry

    for index in range(total // 8):
        state(index, 0)
        for p in range(index * 8 * slots // total, (index + 1) * 8 * slots // total):
            fetch(p)

    for v in range(VARIABLES):
        tile = border[8 * v : 8 * v + 8, :]
        turned[v, 0:LEAD, :] = tile
        turned[v, span - 8 : span, :] = tile
        turned[v, LEAD - WIDTH : LEAD - WIDTH + 8, :] = tile
        turned[v, LEAD + cells_z - WIDTH : LEAD + cells_z - WIDTH + 8, :] = tile
        for begin in range(0, cells_z, LANES):
            turned[v, LEAD + begin : LEAD + begin + LANES, :] = pencils[v, :, begin : begin + LANES].T

    top = jnp.zeros((8, slots), F32)
    for begin in range(0, span, 8):
        parts = [turned[v, begin : begin + 8, :] for v in range(VARIABLES)]
        inverse, pressure = state_of(parts)
        velocity = parts[SPECIES + 2] * inverse
        speed_t[begin : begin + 8, :] = 0.5 * velocity
        press_t[begin : begin + 8, :] = pressure
        size = jnp.abs(velocity)
        if begin < LEAD - WIDTH or begin + 8 > LEAD + cells_z + WIDTH:
            at = begin + lax.broadcasted_iota(jnp.int32, (8, slots), 0)
            size = jnp.where((at >= LEAD - WIDTH) & (at < LEAD + cells_z + WIDTH), size, 0.0)
        top = jnp.maximum(top, size)
    wave = 0.5 * (jnp.max(top, axis=0, keepdims=True) + 1.0)

    def project(index, carry):
        at = pl.ds(pl.multiple_of(index * GROUP, GROUP), GROUP)
        velocity = speed_t[at, :]
        pressure = press_t[at, :]
        parts = [turned[v, at, :] for v in range(VARIABLES)]
        flux = [part * velocity for part in parts]
        flux[SPECIES + 2] = flux[SPECIES + 2] + 0.5 * pressure
        flux[SPECIES + 3] = flux[SPECIES + 3] + pressure * velocity
        high, low = [], []
        for v in range(VARIABLES):
            one, two = split(jnp.concatenate([flux[v], wave * parts[v]], axis=1))
            high.append(one)
            low.append(two)
        high = jnp.concatenate(high, axis=0)
        low = jnp.concatenate(low, axis=0)
        both = dot(left_high, high) + dot(left_high, low) + dot(left_low, high)
        both = both.reshape(VARIABLES, GROUP, 2 * slots)
        g_out[:, at, :] = both[:, :, :slots] + both[:, :, slots:]
        g_in[:, at, :] = both[:, :, :slots] - both[:, :, slots:]
        return carry

    lax.fori_loop(0, span // GROUP, project, 0, unroll=True)

    def upwind(i, carry):
        for side, source in enumerate((g_out, g_in)):
            for begin in range(0, span, 8):
                step = source[i, begin + 1 : begin + 9, :] - source[i, begin : begin + 8, :]
                delta[side, begin : begin + 8, :] = step
                triple[side, begin : begin + 8, :] = 3.0 * step
            for begin in range(1, span, 8):
                bend = delta[side, begin : begin + 8, :] - delta[side, begin - 1 : begin + 7, :]
                curve[side, begin : begin + 8, :] = bend
                smooth[side, begin : begin + 8, :] = (13.0 / 3.0 * bend) * bend + weno_epsilon
            for begin in range(0, span, 8):
                third[side, begin : begin + 8, :] = (
                    curve[side, begin + 1 : begin + 9, :] - curve[side, begin : begin + 8, :]
                )
        for begin in range(0, cells_z + 8, 8):
            at = begin + LEAD - 1

            def read(ref, side, offset):
                return ref[side, at + offset : at + offset + 8, :]

            value = None
            for side, source in enumerate((g_out, g_in)):
                if side == 0:
                    d1, d2, d3, d4 = (read(delta, 0, o) for o in (-2, -1, 0, 1))
                    three2, three3 = read(triple, 0, -1), read(triple, 0, 0)
                    s1, s2, s3 = (read(smooth, 0, o) for o in (-1, 0, 1))
                    u1, u2 = (read(third, 0, o) for o in (-1, 0))
                else:
                    d1, d2, d3, d4 = (read(delta, 1, o) for o in (2, 1, 0, -1))
                    three2, three3 = read(triple, 1, 1), read(triple, 1, 0)
                    s1, s2, s3 = (read(smooth, 1, o) for o in (2, 1, 0))
                    u1, u2 = (read(third, 1, o) for o in (1, 0))
                centre = source[i, at + side : at + side + 8, :]
                t0 = three2 - d1
                t1 = d2 + d3
                t2 = d4 - three3
                r0 = pl.reciprocal(s1 + t0 * t0, approx=True)
                r1 = pl.reciprocal(s2 + t1 * t1, approx=True)
                r2 = pl.reciprocal(s3 + t2 * t2, approx=True)
                w0 = r0 * (r0 * (1.0 / 3.0))
                w1 = r1 * r1
                w2 = r2 * r2
                above = (w0 + w0) * u1 + w2 * u2
                below = (w0 + w2) + (w1 + w1)
                bent = above * pl.reciprocal(below, approx=True)
                line = t1 + d3
                if side == 0:
                    value = 6.0 * centre + line - bent
                else:
                    value = value + (6.0 * centre - line + bent)
            faces[i, begin : begin + 8, :] = value
        return carry

    lax.fori_loop(0, VARIABLES, upwind, 0)

    keep = wanted >= 0

    def back(index, carry):
        base = pl.multiple_of(index * 2 * GROUP, 2 * GROUP)
        high, low = [], []
        for v in range(VARIABLES):
            pieces = []
            for begin in (0, GROUP):
                here = faces[v, pl.ds(base + begin, GROUP), :]
                after = faces[v, pl.ds(base + begin + 1, GROUP), :]
                pieces.append(after - here)
            one, two = split(jnp.concatenate(pieces, axis=1))
            high.append(one)
            low.append(two)
        high = jnp.concatenate(high, axis=0)
        low = jnp.concatenate(low, axis=0)
        both = dot(right_high, high) + dot(right_high, low) + dot(right_low, high)
        both = both.reshape(VARIABLES, GROUP, 2 * slots)
        for part, begin in enumerate((0, GROUP)):
            piece = jnp.where(keep[None], both[:, :, part * slots : part * slots + slots], 0.0)
            one, two = split(piece)
            change_ref[:, pl.ds(base + begin, GROUP), :slots] = one
            change_ref[:, pl.ds(base + begin, GROUP), slots:] = two
        return carry

    lax.fori_loop(0, cells_z // (2 * GROUP), back, 0, unroll=True)


def shock(wanted, conserved, face, basis):
    _, cells_x, cells_y, cells_z = conserved.shape
    slots = wanted.shape[-1]
    total = cells_x * cells_y
    span = -(-(cells_z + 2 * LEAD) // GROUP) * GROUP
    vmem = pltpu.VMEM
    work = vmem((2, span + 8, slots), F32)
    scratch = [
        vmem((VARIABLES, slots, cells_z), F32),
        vmem((VARIABLES, span, slots), F32),
        vmem((span, slots), F32),
        vmem((span, slots), F32),
        vmem((VARIABLES, span + 8, slots), F32),
        vmem((VARIABLES, span + 8, slots), F32),
        work,
        work,
        work,
        work,
        work,
        vmem((VARIABLES, cells_z + 8, slots), F32),
        vmem((LANES, total), F32),
    ]
    smem = pl.BlockSpec(memory_space=pltpu.SMEM)
    whole = pl.BlockSpec(memory_space=pltpu.VMEM)
    return pl.pallas_call(
        shock_kernel,
        out_shape=[
            jax.ShapeDtypeStruct((VARIABLES, cells_z, 2 * slots), BF16),
            jax.ShapeDtypeStruct((total, 2 * slots), BF16),
            jax.ShapeDtypeStruct((total, LANES), F32),
            jax.ShapeDtypeStruct((4, total, cells_z), F32),
        ],
        in_specs=[smem, whole, whole, whole, whole],
        out_specs=[whole] * 4,
        scratch_shapes=scratch,
        compiler_params=pltpu.CompilerParams(vmem_limit_bytes=24 << 20),
        cost_estimate=pl.CostEstimate(flops=100_000_000, bytes_accessed=1_000_000, transcendentals=0),
        name="shock",
    )(wanted, wanted, conserved, face, basis)


def advance_kernel(
    u_ref, change_ref, hot_ref, edge_ref, state_ref, before_ref, after_ref, out_ref, done, left, right, rim, out_sem
):
    _, total, cells_z = u_ref.shape
    cells_x = before_ref.shape[2]
    cells_y = total // cells_x
    halves = cells_z // LANES
    scale = time_step / 60.0
    rows = right.shape[2] // 2 - cells_z

    row = lax.broadcasted_iota(jnp.int32, (cells_z, cells_z), 0)
    column = lax.broadcasted_iota(jnp.int32, (cells_z, cells_z), 1)
    along_z = stencil(row - column).astype(BF16)
    row = lax.broadcasted_iota(jnp.int32, (rows, rows), 0)
    column = lax.broadcasted_iota(jnp.int32, (rows, rows), 1)
    inside = row // cells_y == column // cells_y
    along_y = jnp.where(inside, stencil(column - row), 0.0).astype(BF16)
    for turn in range(1):
        for block in range(total // rows):
            for k in range(2):
                left[turn, block, :, 2 * cells_z + k * rows : 2 * cells_z + k * rows + rows] = along_y
                right[turn, block, k * cells_z : k * cells_z + cells_z, :] = along_z

    rim[...] = jnp.zeros_like(rim)
    for half in range(halves):
        wide = slice(half * LANES, half * LANES + LANES)
        f0, f1, f2 = (flux_of([before_ref[j, v, :, wide] for v in range(VARIABLES)], 1) for j in range(WIDTH))
        for v in range(VARIABLES):
            for j, part in enumerate((45.0 * f2[v] - 9.0 * f1[v] + f0[v], f1[v] - 9.0 * f2[v], f2[v])):
                rim[v, half, pl.ds(j, cells_x, stride=2 * GROUP), :] = scale * part
        f0, f1, f2 = (flux_of([after_ref[j, v, :, wide] for v in range(VARIABLES)], 1) for j in range(WIDTH))
        for v in range(VARIABLES):
            for j, part in enumerate((f0[v], f1[v] - 9.0 * f0[v], 45.0 * f0[v] - 9.0 * f1[v] + f2[v])):
                rim[v, half, pl.ds(2 * GROUP - WIDTH + j, cells_x, stride=2 * GROUP), :] = -scale * part

    lane = lax.broadcasted_iota(jnp.int32, (GROUP, LANES), 1)
    for v in range(VARIABLES):
        turn = 0

        for begin in range(0, total, GROUP):
            at = slice(begin, begin + GROUP)
            block, place = begin // rows, begin % rows
            value = u_ref[v, at, :]
            flux_y = value * state_ref[0, at, :]
            flux_z = value * state_ref[1, at, :]
            if v == SPECIES + 1:
                flux_y = flux_y + scale * state_ref[2, at, :]
            if v == SPECIES + 2:
                flux_z = flux_z + state_ref[3, at, :]
            if v == SPECIES + 3:
                flux_y = flux_y + state_ref[2, at, :] * state_ref[0, at, :]
                flux_z = flux_z + state_ref[2, at, :] * state_ref[1, at, :]
            high, low = split(flux_z)
            left[turn, block, place : place + GROUP, :cells_z] = high
            left[turn, block, place : place + GROUP, cells_z : 2 * cells_z] = low
            high, low = split(flux_y)
            place = place + 2 * cells_z
            right[turn, block, place : place + GROUP, :] = high
            right[turn, block, place + rows : place + rows + GROUP, :] = low
        for block in range(total // rows):
            base = block * rows
            gained = dot(left[turn, block], right[turn, block])
            gained = gained + lax.dot_general(
                hot_ref[base : base + rows, :], change_ref[v], (((1,), (1,)), ((), ())), preferred_element_type=F32
            )
            for begin in range(base, base + rows, GROUP):
                at = slice(begin, begin + GROUP)
                x, y = begin // cells_y, begin % cells_y
                border = pltpu.roll(edge_ref[at, :], (LANES - WIDTH - 8 * v) % LANES, 1)
                for half in range(halves):
                    wide = slice(half * LANES, half * LANES + LANES)
                    value = u_ref[v, at, wide] - gained[begin - base : begin - base + GROUP, wide]
                    if half == 0:
                        value = value - jnp.where(lane < WIDTH, border, 0.0)
                    if half == halves - 1:
                        value = value - jnp.where(lane >= LANES - WIDTH, border, 0.0)
                    if y == 0:
                        value = value + rim[v, half, 2 * GROUP * x : 2 * GROUP * x + GROUP, :]
                    if y == cells_y - GROUP:
                        value = value + rim[v, half, 2 * GROUP * x + GROUP : 2 * GROUP * x + 2 * GROUP, :]
                    done[v, at, wide] = value
        pltpu.make_async_copy(done.at[v], out_ref.at[v], out_sem).start()
    pltpu.make_async_copy(done, done, out_sem).wait()


def advance(conserved, change, hot, edge, state, before, after):
    _, cells_x, cells_y, cells_z = conserved.shape
    total = cells_x * cells_y
    rows = cells_y * max(1, min(cells_x, 256 // cells_y))
    whole = pl.BlockSpec(memory_space=pltpu.VMEM)
    result = pl.pallas_call(
        advance_kernel,
        out_shape=jax.ShapeDtypeStruct((VARIABLES, total, cells_z), F32),
        in_specs=[whole] * 7,
        out_specs=pl.BlockSpec(memory_space=pl.ANY),
        scratch_shapes=[
            pltpu.VMEM((VARIABLES, total, cells_z), F32),
            pltpu.VMEM((1, total // rows, rows, 2 * (cells_z + rows)), BF16),
            pltpu.VMEM((1, total // rows, 2 * (cells_z + rows), cells_z), BF16),
            pltpu.VMEM((VARIABLES, cells_z // LANES, cells_x * 2 * GROUP, LANES), F32),
            pltpu.SemaphoreType.DMA(()),
        ],
        compiler_params=pltpu.CompilerParams(vmem_limit_bytes=24 << 20),
        cost_estimate=pl.CostEstimate(flops=4_000_000_000, bytes_accessed=20_000_000, transcendentals=0),
        name="advance",
    )(conserved.reshape(VARIABLES, total, cells_z), change, hot, edge, state, before, after)
    return result.reshape(conserved.shape)


def on_device(conserved, char_left, char_right, shock_list, shock_count):
    count = lax.axis_size("gy")
    ahead = [(i, (i + 1) % count) for i in range(count)]
    tail, head, first = pack_y(conserved)
    before = lax.ppermute(tail, "gy", ahead)
    after = lax.ppermute(head, "gy", [(b, a) for a, b in ahead])
    basis = jnp.stack([0.5 * char_left, (time_step / 3.0) * char_right])
    slots = shock_list.shape[-1]
    wanted = jnp.where(jnp.arange(slots, dtype=jnp.int32) < shock_count, shock_list, -1).reshape(1, slots)
    face = exchange_z(pack_z(conserved, first, basis, wanted))
    change, hot, edge, state = shock(
        wanted, conserved, face, basis
    )
    return advance(conserved, change, hot, edge, state, before, after)


def solution(mesh):
    placed = (P(None, "gx", "gy", "gz"), P(), P(), P("gx", "gy", "gz", None), P("gx", "gy", "gz"))
    return jax.shard_map(
        on_device, mesh=mesh, in_specs=placed, out_specs=P(None, "gx", "gy", "gz"), check_vma=False
    )
```
